256 devices in a mesh: blk: 32 (over z_lo, y, core), row: 8 (over z_hi, x).
Axes of the slice: x: 4, y: 4, z: 8 (z_hi: 2, z_lo: 4; z = z_hi * 4 + z_lo), core: 2. Of those that a mesh axis runs over, the one named last changes fastest.
Arguments:
- features: float32 [16384, 256], P(('blk', 'row')), may hold values from -2 to 2, as said below
- probes: float32 [16384, 128], P(('blk', 'row')), may hold values from -6 to 6
- outputscale: float32 [1], replicated, may hold values from 0.05 to 0.2
- noise: float32 [1], replicated, may hold values from 0.5 to 2
- pivots: int32 [256], replicated, may hold values from 0 to 16383, as said below
Outputs:
- product: float32 [16384, 128], P(('blk', 'row'))
- preconditioned: float32 [16384, 128], P(('blk', 'row'))
The draws below stay inside these ranges and needn't reach their ends.
Inputs may be any that keep to these rules, and one draw needn't show every extreme that they name: `pivots`: 256 distinct point indices. real-valued features.
All inputs are finite; a program needn't handle non-finite values.
Results may differ from the reference program's by a relative error of at most 0.0003.
Values sent between devices are 32-bit elements; how exact they have to be, the bound alone decides.
A program may use at most 64 MiB of HBM per device.

```python
import math
import jax
import jax.numpy as jnp
from jax import lax

F = 256
PROBES = 128
RANK = 256
POINTS = 16384


def draw_pivots(key, part):
    ordering = jax.random.permutation(jax.random.fold_in(key, 7), POINTS)
    return ordering[:RANK].astype(jnp.int32)


def draw_features(key, part):
    key_list = [jax.random.fold_in(key, 101 + position) for position in range(7)]
    centres = 0.8 * jnp.clip(jax.random.normal(key_list[0], (64, 8), jnp.float32), -3.0, 3.0)
    owners = jax.random.randint(key_list[1], (POINTS,), 0, 64)
    offsets = jnp.clip(jax.random.normal(key_list[2], (POINTS, 8), jnp.float32), -3.0, 3.0)
    spread = jnp.exp(jax.random.uniform(key_list[3], (POINTS, 1), jnp.float32, math.log(0.15), math.log(0.6)))
    jitter = jnp.clip(jax.random.normal(key_list[6], (POINTS, F), jnp.float32), -4.0, 4.0)
    latent = centres[owners] + spread * offsets
    mixing = jnp.clip(jax.random.normal(key_list[4], (8, F), jnp.float32), -4.0, 4.0) / math.sqrt(F)
    bending = jnp.clip(jax.random.normal(key_list[5], (8, F), jnp.float32), -4.0, 4.0) / math.sqrt(8.0)
    linear_part = jnp.dot(latent, mixing, precision=lax.Precision.HIGHEST, preferred_element_type=jnp.float32)
    curved_part = jnp.tanh(jnp.dot(latent, bending, precision=lax.Precision.HIGHEST, preferred_element_type=jnp.float32))
    result_feats = linear_part + 0.7 / math.sqrt(F) * curved_part + 0.34 / math.sqrt(F) * jitter
    return jnp.clip(result_feats, -2.0, 2.0).astype(jnp.float32)


def steps_of(own_key, extent, shards, smallest, top_value):
    def one(dim, shards_of):
        steps = jax.random.uniform(jax.random.fold_in(jax.random.fold_in(own_key, 6), dim), (shards_of,), jnp.float32, smallest / len(shards), top_value / len(shards))
        return jnp.repeat(jnp.exp(steps), extent[dim] // shards_of).reshape((-1,) + (1,) * (len(extent) - dim - 1))

    level = one(*shards[0])
    for cut in shards[1:]:
        level = level * one(*cut)
    return level


def normal_values(own_key, shape, scale, limit, shards=(), held_as=jnp.bfloat16):
    drawn = scale * jax.random.normal(own_key, shape, jnp.float32)
    if shards:
        drawn = drawn * steps_of(own_key, shape, shards, -0.22, 0.18)
    return jnp.clip(drawn, -limit, limit).astype(held_as)


def setup_inputs(seed: int = 0) -> dict:
    key_of = jax.random.split(jax.random.key(seed), 6)
    return {
        "features": draw_features(jax.random.fold_in(key_of[5], 71), 0),
        "probes": normal_values(key_of[1], (POINTS, PROBES), 1.0, 6.0, ((0, 256),), jnp.float32),
        "outputscale": jnp.clip(jnp.exp(jax.random.uniform(key_of[2], (1,), jnp.float32, math.log(0.05), math.log(0.2))), 0.05, 0.2),
        "noise": jnp.clip(jnp.exp(jax.random.uniform(key_of[3], (1,), jnp.float32, math.log(0.5), math.log(2.0))), 0.5, 2.0),
        "pivots": draw_pivots(jax.random.fold_in(key_of[5], 71), 0),
    }


highest = lax.Precision.HIGHEST
root_five = 2.23606797749979

def kernel_tile(row_feats, row_norms, col_feats, col_norms):
    inner = lax.dot_general(row_feats.astype(jnp.float32), col_feats.astype(jnp.float32), (((1,), (1,)), ((), ())), precision=highest, preferred_element_type=jnp.float32)
    squared = jnp.maximum(row_norms[:, None] + col_norms[None, :] - 2.0 * inner, 0.0)
    scaled = root_five * jnp.sqrt(squared)
    return (1.0 + scaled + scaled * scaled / 3.0) * jnp.exp(-scaled)

def reference(features, probes, outputscale, noise, pivots):
    total_points, feature_count = features.shape
    amplitude = outputscale[0]
    nugget = noise[0]
    norms = lax.optimization_barrier(jnp.sum(features * features, axis=1))
    span = math.gcd(total_points, 1024)

    def one_block(inputs):
        block_feats, block_norms = inputs
        kernel_block = kernel_tile(block_feats, block_norms, features, norms)
        return jnp.dot(kernel_block.astype(jnp.float32), probes.astype(jnp.float32), precision=highest, preferred_element_type=jnp.float32)
    kernel_probes = lax.map(one_block, (features.reshape(-1, span, feature_count), norms.reshape(-1, span)))
    kernel_probes = kernel_probes.reshape(total_points, -1)
    product = amplitude * kernel_probes + nugget * probes
    pivot_feats = features[pivots]
    pivot_norms = lax.optimization_barrier(jnp.sum(pivot_feats * pivot_feats, axis=1))
    cross = amplitude * kernel_tile(features, norms, pivot_feats, pivot_norms)
    inner_pivots = amplitude * kernel_tile(pivot_feats, pivot_norms, pivot_feats, pivot_norms)
    gram = nugget * inner_pivots + lax.dot_general(cross.astype(jnp.float32), cross.astype(jnp.float32), (((0,), (0,)), ((), ())), precision=highest, preferred_element_type=jnp.float32)
    projected = lax.dot_general(cross.astype(jnp.float32), product.astype(jnp.float32), (((0,), (0,)), ((), ())), precision=highest, preferred_element_type=jnp.float32)
    factor = jnp.linalg.cholesky(gram)
    coefficients = jax.scipy.linalg.cho_solve((factor, True), projected)
    preconditioned = (product - jnp.dot(cross.astype(jnp.float32), coefficients.astype(jnp.float32), precision=highest, preferred_element_type=jnp.float32)) / nugget
    return (product, preconditioned)
```

```python
import functools

import jax
import jax.numpy as jnp
from jax import lax
from jax.experimental import pallas as pl
from jax.experimental.pallas import tpu as pltpu
from jax.sharding import PartitionSpec as P

MESH = pl.DeviceIdType.MESH
highest = lax.Precision.HIGHEST
root_five = 2.23606797749979
f32 = jnp.float32
bf16 = jnp.bfloat16

NX, NY, NZ, NC = 4, 4, 8, 2
ZLO = 4
PLANE = NX * NY
LINE = NZ * NC


def split(x):
    hi = x.astype(bf16)
    return hi, (x - hi.astype(f32)).astype(bf16)


def dot_nt(a, b):
    return lax.dot_general(a, b, (((1,), (1,)), ((), ())), preferred_element_type=f32)


def dot_nn(a, b):
    return jnp.dot(a, b, preferred_element_type=f32)


def matern(scaled_square):
    s = jnp.maximum(scaled_square, 1e-30)
    t = s * lax.rsqrt(s)
    return (1.0 + t + s * (1.0 / 3.0)) * jnp.exp(-t)


def row_norms(x):
    ones = jnp.ones((8, x.shape[1]), f32)
    return lax.dot_general(
        ones, x * x, (((1,), (1,)), ((), ())), precision=highest, preferred_element_type=f32
    )[0:1]


def column_norms(x):
    return jnp.broadcast_to(jnp.sum(x * x, axis=1, keepdims=True), (x.shape[0], 128))


def twice(x):
    return jnp.concatenate([x, x], axis=1)


def exchange_kernel(
    feats_ref, probes_ref, pivots_ref, amp_ref, noise_ref,
    product_ref, proj_ref, gram_ref, cross_ref,
    a_buf, b_buf, pick, p1_buf, p2_src, p2_buf, piv,
    r_cat, r_norm, r_norm_row, c_cat, c_norm_row, v_cat, part,
    piv_cat, piv_rcat, ct_hi, ct_lo, g_src, g_buf, gram, q_all, q1_buf, q_src, q_buf, q_out, prod_buf,
    a_sem, b_sem, p1_sem, p2_sem, p3_sem, g1_sem, g2_sem, r_sem, q1_sem, q2_sem, q3_sem,
):
    n_rows, n_feat = feats_ref.shape
    n_probe = probes_ref.shape[1]
    rank = pivots_ref.shape[0]
    chunk = rank // PLANE
    blk, row = lax.axis_index("blk"), lax.axis_index("row")
    core = lax.rem(blk, NC)
    y = lax.rem(lax.div(blk, NC), NY)
    x = lax.rem(row, NX)
    z = lax.div(row, NX) * ZLO + lax.div(blk, NC * NY)
    here = y * NX + x

    def plane(dx, dy):
        xx, yy = lax.rem(x + (dx + NX), NX), lax.rem(y + (dy + NY), NY)
        return ((lax.div(blk, NC * NY) * NY + yy) * NC + core, lax.div(row, NX) * NX + xx), yy * NX + xx

    def line(dz, dc):
        zz, cc = lax.rem(z + (dz + NZ), NZ), lax.rem(core + dc, NC)
        return ((lax.rem(zz, ZLO) * NY + y) * NC + cc, lax.div(zz, ZLO) * NX + x)

    plane_offsets = sorted(
        [(dx, dy) for dx in range(NX) for dy in range(NY) if dx or dy],
        key=lambda o: min(o[0], NX - o[0]) + min(o[1], NY - o[1]),
    )
    line_offsets = sorted(
        [(dz, dc) for dz in range(NZ) for dc in range(NC) if dz or dc],
        key=lambda o: min(o[0], NZ - o[0]),
    )

    def send(src, dst, sem, k, device):
        copy = pltpu.make_async_remote_copy(
            src_ref=src, dst_ref=dst, send_sem=sem.at[0, k], recv_sem=sem.at[1, k],
            device_id=device, device_id_type=MESH,
        )
        copy.start()
        return copy

    barrier = pltpu.get_barrier_semaphore()
    for dx, dy in plane_offsets:
        pl.semaphore_signal(barrier, inc=1, device_id=plane(dx, dy)[0], device_id_type=MESH)
    for dz, dc in line_offsets:
        pl.semaphore_signal(barrier, inc=1, device_id=line(dz, dc), device_id_type=MESH)

    amp, noise = amp_ref[0], noise_ref[0]
    own = feats_ref[...] * root_five
    a_buf[0] = own
    b_buf[0, :, :n_feat] = own
    b_buf[0, :, n_feat:] = probes_ref[...]
    first = (blk * (NX * NZ // ZLO) + row) * n_rows
    local = lax.broadcasted_iota(jnp.int32, (rank, n_rows), 1) + first
    onehot = (local == pivots_ref[:, :n_rows]).astype(f32)
    pick[...] = lax.dot_general(
        onehot, own, (((1,), (0,)), ((), ())), precision=highest, preferred_element_type=f32
    )
    pl.semaphore_wait(barrier, PLANE + LINE - 2)

    def mine(ref):
        return ref.at[pl.ds(pl.multiple_of(here * chunk, chunk), chunk)]

    def plane_scatter(src, dst, sem):
        copies = []
        for dx, dy in plane_offsets:
            device, there = plane(dx, dy)
            k = dy * NX + dx
            source = src.at[pl.ds(pl.multiple_of(there * chunk, chunk), chunk)]
            copies.append(send(source, dst.at[k], sem, k, device))
        return copies

    def plane_gather(ref, sem):
        copies = []
        for dx, dy in plane_offsets:
            k = dy * NX + dx
            copies.append(send(mine(ref), mine(ref), sem, k, plane(dx, dy)[0]))
        return copies

    def line_gather(src, dst, sem):
        copies = []
        for dz, dc in line_offsets:
            k = dz * NC + dc
            copies.append(send(src, dst.at[k], sem, k, line(dz, dc)))
        return copies

    def landed(copies):
        for c in copies:
            c.wait_recv()

    def summed(own_value, buf, count):
        total = own_value
        for k in range(1, count):
            total = total + buf[k]
        return total

    everything = []

    p1 = plane_scatter(pick, p1_buf, p1_sem)

    half = n_rows // 2
    right, left = line(1, 0), line(-1, 0)
    sibling = line(0, 1)

    def b_slot(dz, dc):
        return b_buf.at[dz * NC + dc]

    def b_send(dz_from, dz_to, device):
        return send(b_slot(dz_from, 0), b_slot(dz_to, 0), b_sem, dz_to * NC, device)

    def b_sibling(dz):
        return send(b_slot(dz, 0), b_slot(dz, 1), b_sem, dz * NC + 1, sibling)

    ring = {1: b_send(0, 1, right), 7: b_send(0, 7, left)}
    across = {0: b_sibling(0)}

    a_copies = []
    for dx, dy in plane_offsets:
        k = dy * NX + dx
        a_copies.append(send(a_buf.at[0], a_buf.at[k], a_sem, k, plane(dx, dy)[0]))

    landed(p1)
    p2_src[...] = summed(pick[pl.ds(pl.multiple_of(here * chunk, chunk), chunk), :], p1_buf, PLANE)
    p2 = line_gather(p2_src, p2_buf, p2_sem)

    def forward(step):
        ring[step].wait_recv()
        ring[8 - step].wait_recv()
        if step < 3:
            ring[step + 1] = b_send(step, step + 1, right)
            ring[7 - step] = b_send(8 - step, 7 - step, left)
        else:
            lower, upper = pl.ds(0, half), pl.ds(half, half)
            ring[4] = send(b_slot(3, 0).at[lower], b_slot(4, 0).at[lower], b_sem, 8, right)
            ring["4b"] = send(b_slot(5, 0).at[upper], b_slot(4, 0).at[upper], b_sem, LINE, left)
        across[step] = b_sibling(step)
        across[8 - step] = b_sibling(8 - step)

    forward(1)

    landed(p2)
    piv_rows = pl.ds(pl.multiple_of(here * chunk, chunk), chunk)
    piv[piv_rows, :] = summed(p2_src[...], p2_buf, LINE)
    p3 = plane_gather(piv, p3_sem)

    forward(2)

    landed(a_copies)

    for k in range(PLANE):
        rows = slice(k * n_rows, (k + 1) * n_rows)
        value = a_buf[k]
        hi, lo = split(value * -2.0)
        r_cat[rows, :n_feat] = hi
        r_cat[rows, n_feat:2 * n_feat] = hi
        r_cat[rows, 2 * n_feat:] = lo
        r_norm[rows, :] = column_norms(value)
    for k in range(0, PLANE, 4):
        value = a_buf[pl.ds(k, 4)].reshape(4 * n_rows, n_feat)
        r_norm_row[:, k * n_rows:(k + 4) * n_rows] = row_norms(value)

    part[...] = jnp.zeros_like(part)
    width = 4 * n_rows
    tile = 256

    def columns(slots):
        for i, (dz, dc) in enumerate(slots):
            rows = slice(i * n_rows, (i + 1) * n_rows)
            value = b_buf[dz * NC + dc, :, :n_feat]
            hi, lo = split(value)
            c_cat[rows, :n_feat] = hi
            c_cat[rows, n_feat:2 * n_feat] = lo
            c_cat[rows, 2 * n_feat:] = hi
            hi, lo = split(b_buf[dz * NC + dc, :, n_feat:])
            v_cat[rows, :n_probe] = hi
            v_cat[rows, n_probe:] = lo
            c_norm_row[:, rows] = row_norms(value)

        def body(i, carry):
            rows = pl.ds(pl.multiple_of(i * tile, tile), tile)
            s = dot_nt(r_cat[rows, :], c_cat[...])
            k = matern(s + twice(r_norm[rows, :]) + c_norm_row[...])
            hi, lo = split(k)
            both = dot_nn(hi, v_cat[...])
            last = dot_nn(lo, v_cat[:, :n_probe])
            part[rows, :] = part[rows, :] + (both[:, :n_probe] + both[:, n_probe:] + last)
            return carry

        lax.fori_loop(0, part.shape[0] // tile, body, 0)

    across[0].wait_recv()
    across[1].wait_recv()
    columns([(0, 0), (0, 1), (1, 0), (1, 1)])

    forward(3)

    landed(p3)
    pv = piv[...]
    hi, lo = split(pv)
    piv_cat[:, :n_feat] = hi
    piv_cat[:, n_feat:2 * n_feat] = lo
    piv_cat[:, 2 * n_feat:] = hi
    hi, lo = split(pv * -2.0)
    piv_rcat[:, :n_feat] = hi
    piv_rcat[:, n_feat:2 * n_feat] = hi
    piv_rcat[:, 2 * n_feat:] = lo
    piv_norm = column_norms(pv)
    piv_norm_row = row_norms(pv)
    for i in range(r_cat.shape[0] // tile):
        rows = slice(i * tile, (i + 1) * tile)
        s = dot_nt(piv_cat[...], r_cat[rows, :])
        ct = amp * matern(s + twice(piv_norm) + r_norm_row[:, rows])
        hi, lo = split(ct)
        ct_hi[:, rows] = hi
        ct_lo[:, rows] = lo
    g_hi, g_lo = ct_hi[piv_rows, :], ct_lo[piv_rows, :]
    g_src[...] = dot_nt(g_hi, ct_hi[...]) + dot_nt(g_hi, ct_lo[...]) + dot_nt(g_lo, ct_hi[...])
    g1 = line_gather(g_src, g_buf, g1_sem)

    s = dot_nt(r_cat[:n_rows, :], piv_cat[...])
    cross_ref[...] = amp * matern(s + twice(r_norm[:n_rows, :]) + piv_norm_row)

    across[2].wait_recv()
    across[7].wait_recv()
    columns([(7, 0), (7, 1), (2, 0), (2, 1)])

    landed(g1)
    gram[piv_rows, :] = summed(g_src[...], g_buf, LINE)
    g2 = plane_gather(gram, g2_sem)

    ring[4].wait_recv()
    ring["4b"].wait_recv()
    across[4] = b_sibling(4)

    across[6].wait_recv()
    across[3].wait_recv()
    columns([(6, 0), (6, 1), (3, 0), (3, 1)])
    across[5].wait_recv()
    across[4].wait_recv()
    columns([(5, 0), (5, 1), (4, 0), (4, 1)])

    part[...] = part[...] * amp
    part[:n_rows, :] = part[:n_rows, :] + noise * probes_ref[...]
    r_copies = []
    for dx, dy in plane_offsets:
        k = dy * NX + dx
        source = part.at[pl.ds(k * n_rows, n_rows)]
        r_copies.append(send(source, prod_buf.at[k], r_sem, k, plane(-dx, -dy)[0]))

    hi, lo = split(part[...])
    both = dot_nn(ct_hi[...], jnp.concatenate([hi, lo], axis=1))
    q_all[...] = both[:, :n_probe] + both[:, n_probe:] + dot_nn(ct_lo[...], hi)
    q1 = plane_scatter(q_all, q1_buf, q1_sem)
    landed(q1)
    q_src[...] = summed(q_all[piv_rows, :], q1_buf, PLANE)
    q2 = line_gather(q_src, q_buf, q2_sem)

    s = dot_nt(piv_rcat[...], piv_cat[...])
    inner = (noise * amp) * matern(s + twice(piv_norm) + piv_norm_row)

    landed(r_copies)
    product_ref[...] = summed(part[:n_rows, :], prod_buf, PLANE)

    landed(q2)
    q_out[piv_rows, :] = summed(q_src[...], q_buf, LINE)
    q3 = plane_gather(q_out, q3_sem)
    landed(g2)
    gram_ref[...] = gram[...] + inner
    landed(q3)
    proj_ref[...] = q_out[...]

    for group in (p1, p2, p3, g1, g2, q1, q2, q3, r_copies, a_copies, ring.values(), across.values()):
        for c in group:
            c.wait_send()


def per_device(features, probes, outputscale, noise, pivots):
    n_rows, n_feat = features.shape
    n_probe = probes.shape[1]
    rank = pivots.shape[0]
    chunk = rank // PLANE
    wide = PLANE * n_rows
    block = 4 * n_rows
    vmem = pltpu.VMEM
    dma = pltpu.SemaphoreType.DMA
    spread = jnp.broadcast_to(pivots[:, None], (rank, 128))
    product, projected, gram, cross = pl.pallas_call(
        exchange_kernel,
        out_shape=(
            jax.ShapeDtypeStruct((n_rows, n_probe), f32),
            jax.ShapeDtypeStruct((rank, n_probe), f32),
            jax.ShapeDtypeStruct((rank, rank), f32),
            jax.ShapeDtypeStruct((n_rows, rank), f32),
        ),
        in_specs=[pl.BlockSpec(memory_space=vmem)] * 3
        + [pl.BlockSpec(memory_space=pltpu.SMEM)] * 2,
        out_specs=[pl.BlockSpec(memory_space=vmem)] * 4,
        scratch_shapes=[
            vmem((PLANE, n_rows, n_feat), f32),
            vmem((LINE, n_rows, n_feat + n_probe), f32),
            vmem((rank, n_feat), f32),
            vmem((PLANE, chunk, n_feat), f32),
            vmem((chunk, n_feat), f32),
            vmem((LINE, chunk, n_feat), f32),
            vmem((rank, n_feat), f32),
            vmem((wide, 3 * n_feat), bf16),
            vmem((wide, 128), f32),
            vmem((1, wide), f32),
            vmem((block, 3 * n_feat), bf16),
            vmem((1, block), f32),
            vmem((block, 2 * n_probe), bf16),
            vmem((wide, n_probe), f32),
            vmem((rank, 3 * n_feat), bf16),
            vmem((rank, 3 * n_feat), bf16),
            vmem((rank, wide), bf16),
            vmem((rank, wide), bf16),
            vmem((chunk, rank), f32),
            vmem((LINE, chunk, rank), f32),
            vmem((rank, rank), f32),
            vmem((rank, n_probe), f32),
            vmem((PLANE, chunk, n_probe), f32),
            vmem((chunk, n_probe), f32),
            vmem((LINE, chunk, n_probe), f32),
            vmem((rank, n_probe), f32),
            vmem((PLANE, n_rows, n_probe), f32),
        ]
        + [dma((2, PLANE)), dma((2, LINE + 1)), dma((2, PLANE)), dma((2, LINE)), dma((2, PLANE))]
        + [dma((2, LINE)), dma((2, PLANE)), dma((2, PLANE)), dma((2, PLANE)), dma((2, LINE)), dma((2, PLANE))],
        compiler_params=pltpu.CompilerParams(
            collective_id=0, has_side_effects=True, vmem_limit_bytes=40 * 1024 * 1024
        ),
        name="exchange",
    )(features, probes, spread, outputscale, noise)
    nugget = noise[0]
    factor = jnp.linalg.cholesky(gram)
    coefficients = jax.scipy.linalg.cho_solve((factor, True), projected)
    preconditioned = (
        product - jnp.dot(cross, coefficients, precision=highest, preferred_element_type=f32)
    ) / nugget
    return product, preconditioned


def solution(mesh):
    in_specs = (P(("blk", "row"), None), P(("blk", "row"), None), P(), P(), P())
    out_specs = (P(("blk", "row"), None), P(("blk", "row"), None))
    return jax.shard_map(
        per_device, mesh=mesh, in_specs=in_specs, out_specs=out_specs, check_vma=False
    )
```

```python
import jax
import jax.numpy as jnp
from jax import lax
from jax.experimental import pallas as pl
from jax.experimental.pallas import tpu as pltpu
from jax.sharding import PartitionSpec as P

MESH = pl.DeviceIdType.MESH
highest = lax.Precision.HIGHEST
root_five = 2.23606797749979
f32 = jnp.float32
bf16 = jnp.bfloat16

NX, NY, NZ, NC = 4, 4, 8, 2
ZLO = 4
PLANE = NX * NY
LINE = NZ * NC


def split(x):
    hi = x.astype(bf16)
    return hi, (x - hi.astype(f32)).astype(bf16)


def dot_nt(a, b):
    return lax.dot_general(a, b, (((1,), (1,)), ((), ())), preferred_element_type=f32)


def dot_nn(a, b):
    return jnp.dot(a, b, preferred_element_type=f32)


def matern(scaled_square):
    s = jnp.maximum(scaled_square, 1e-30)
    t = s * lax.rsqrt(s)
    return (1.0 + t + s * (1.0 / 3.0)) * jnp.exp(-t)


def column_norms(x):
    return jnp.broadcast_to(jnp.sum(x * x, axis=1, keepdims=True), (x.shape[0], 128))


def as_row(norms):
    return jnp.transpose(norms)[0:1]


def twice(x):
    return jnp.concatenate([x, x], axis=1)


def dot_exact(a, b):
    return jnp.dot(a, b, precision=highest, preferred_element_type=f32)


def invert(work, first_tile, last_tile):
    tiles, _, half = work.shape
    sub = lax.broadcasted_iota(jnp.int32, (8, half), 0)
    lane = lax.broadcasted_iota(jnp.int32, (8, half), 1)

    def spread_lane(v, index):
        return jnp.take_along_axis(v, index, axis=1)

    def spread_row(v, r):
        return jnp.broadcast_to(v[r:r + 1, :], v.shape)

    def reciprocal(d):
        r = pl.reciprocal(d, approx=True)
        r = r * (2.0 - d * r)
        return r * (2.0 - d * r)

    def step(kb, carry):
        start = kb * 8
        index = [jnp.full((8, half), start + c, jnp.int32) for c in range(8)]
        active = (lane >= start) & (lane < start + 8)
        top = work[kb]
        d = [spread_lane(top, index[c]) for c in range(8)]
        top = jnp.where(active, jnp.where(lane - start == sub, 1.0, 0.0), top)
        for s in range(0, 8, 2):
            a, b, c = spread_row(d[s], s), spread_row(d[s + 1], s), spread_row(d[s + 1], s + 1)
            inverse = reciprocal(a * c - b * b)
            a, b, c = a * inverse, b * inverse, c * inverse
            first, second = d[s], d[s + 1]

            def swept(v):
                r0, r1 = spread_row(v, s), spread_row(v, s + 1)
                p0 = c * r0 - b * r1
                p1 = a * r1 - b * r0
                rest = v - first * p0 - second * p1
                return jnp.where(sub == s, p0, jnp.where(sub == s + 1, p1, rest))

            for c2 in range(s + 2, 8):
                d[c2] = swept(d[c2])
            top = swept(top)
        rows = [spread_row(top, c) for c in range(8)]
        for r in range(tiles):
            v = work[r]
            total = jnp.where(active, 0.0, v)
            for c in range(8):
                total = total - spread_lane(v, index[c]) * rows[c]
            work[r] = total
        work[kb] = top
        return carry

    lax.fori_loop(first_tile, last_tile, step, 0)


def exchange_kernel(
    feats_ref, probes_ref, pivots_ref, amp_ref, noise_ref,
    product_ref, out_ref,
    a_buf, b_buf, pick, p_buf, piv,
    r_cat, r_norm, r_norm_row, c_cat, c_norm_row, v_cat, part,
    piv_cat, ct, ct_hi, ct_lo, cross_own, g_src, g_buf, gram, q_all, q1_buf, q_src, q_buf, q_out, prod_buf, work, full,
    a_sem, b_sem, p_sem, g_sem, q_sem, q1_sem, r_sem,
):
    n_rows, n_feat = feats_ref.shape
    n_probe = probes_ref.shape[1]
    rank = pivots_ref.shape[0]
    half_rank = rank // NC
    chunk = half_rank // PLANE
    half_feat = n_feat // 2
    blk, row = lax.axis_index("blk"), lax.axis_index("row")
    core = lax.rem(blk, NC)
    y = lax.rem(lax.div(blk, NC), NY)
    x = lax.rem(row, NX)
    z = lax.div(row, NX) * ZLO + lax.div(blk, NC * NY)
    here = y * NX + x

    def plane(dx, dy):
        xx, yy = lax.rem(x + (dx + NX), NX), lax.rem(y + (dy + NY), NY)
        return ((lax.div(blk, NC * NY) * NY + yy) * NC + core, lax.div(row, NX) * NX + xx), yy * NX + xx

    def line(dz, dc):
        zz, cc = lax.rem(z + (dz + NZ), NZ), lax.rem(core + dc, NC)
        return ((lax.rem(zz, ZLO) * NY + y) * NC + cc, lax.div(zz, ZLO) * NX + x), cc

    plane_offsets = sorted(
        [(dx, dy) for dx in range(NX) for dy in range(NY) if dx or dy],
        key=lambda o: -(min(o[0], NX - o[0]) + min(o[1], NY - o[1])),
    )
    line_offsets = sorted(
        [(dz, dc) for dz in range(NZ) for dc in range(NC) if dz or dc],
        key=lambda o: -min(o[0], NZ - o[0]),
    )

    everything = []

    def send(src, dst, sem, k, device):
        copy = pltpu.make_async_remote_copy(
            src_ref=src, dst_ref=dst, send_sem=sem.at[0, k], recv_sem=sem.at[1, k],
            device_id=device, device_id_type=MESH,
        )
        copy.start()
        everything.append(copy)
        return copy

    barrier = pltpu.get_barrier_semaphore()
    for dx, dy in plane_offsets:
        pl.semaphore_signal(barrier, inc=1, device_id=plane(dx, dy)[0], device_id_type=MESH)
    for dz, dc in line_offsets:
        pl.semaphore_signal(barrier, inc=1, device_id=line(dz, dc)[0], device_id_type=MESH)

    amp, noise = amp_ref[0], noise_ref[0]
    own = feats_ref[...] * root_five
    a_buf[0, 0, 0] = own[:, :half_feat]
    a_buf[1, 0, 0] = own[:, half_feat:]
    b_buf[0, :, :n_feat] = own
    b_buf[0, :, n_feat:] = probes_ref[...]
    pl.semaphore_wait(barrier, PLANE + LINE - 2)

    def landed(copies):
        for c in copies:
            c.wait_recv()

    upper_rows, lower_rows = pl.ds(0, n_rows // 2), pl.ds(n_rows // 2, n_rows // 2)

    moved = {}

    def a_slot(h, u, v):
        return a_buf.at[(h, v, u) if h == 0 else (h, u, v)]

    def a_send(h, u, v, du, dv, part_of=None):
        to = ((u + du) % 4, (v + dv) % 4)
        src, dst = a_slot(h, u, v), a_slot(h, *to)
        if part_of is not None:
            src, dst = src.at[part_of], dst.at[part_of]
        index = 2 * (16 * h + 4 * to[0] + to[1]) + (part_of is lower_rows)
        device = plane(du, dv)[0] if h == 0 else plane(dv, du)[0]
        moved[(h, *to, part_of is lower_rows)] = send(src, dst, a_sem, index, device)

    def a_wait(*slots):
        for u, v in slots:
            for h in range(2):
                for low in (False, True):
                    if (h, u, v, low) in moved:
                        moved[(h, u, v, low)].wait_recv()

    def a_round(step):
        for h in range(2):
            if step == 0:
                for d in (1, -1):
                    a_send(h, 0, 0, d, 0)
                    a_send(h, 0, 0, 0, d)
            if step == 1:
                a_send(h, 1, 0, 1, 0, upper_rows)
                a_send(h, 3, 0, -1, 0, lower_rows)
                for u in (1, 3):
                    for d in (1, -1):
                        a_send(h, u, 0, 0, d)
                a_send(h, 0, 1, 0, 1, upper_rows)
                a_send(h, 0, 3, 0, -1, lower_rows)
            if step == 2:
                for d in (1, -1):
                    a_send(h, 2, 0, 0, d)
                for u in (1, 3):
                    a_send(h, u, 1, 0, 1, upper_rows)
                    a_send(h, u, 3, 0, -1, lower_rows)
            if step == 3:
                a_send(h, 2, 1, 0, 1, upper_rows)
                a_send(h, 2, 3, 0, -1, lower_rows)

    right, left = line(1, 0)[0], line(-1, 0)[0]
    sibling = line(0, 1)[0]

    def b_slot(dz, dc):
        return b_buf.at[dz * NC + dc]

    def b_send(dz_from, dz_to, device):
        return send(b_slot(dz_from, 0), b_slot(dz_to, 0), b_sem, dz_to * NC, device)

    def b_sibling(dz):
        return send(b_slot(dz, 0), b_slot(dz, 1), b_sem, dz * NC + 1, sibling)

    def forward(step):
        ring[step].wait_recv()
        ring[8 - step].wait_recv()
        if step < 3:
            ring[step + 1] = b_send(step, step + 1, right)
            ring[7 - step] = b_send(8 - step, 7 - step, left)
        else:
            ring[4] = send(b_slot(3, 0).at[upper_rows], b_slot(4, 0).at[upper_rows], b_sem, 8, right)
            ring["4b"] = send(b_slot(5, 0).at[lower_rows], b_slot(4, 0).at[lower_rows], b_sem, LINE, left)
        across[step] = b_sibling(step)
        across[8 - step] = b_sibling(8 - step)

    def prepare(slots):
        for dx, dy in slots:
            k = dy * NX + dx
            rows = slice(k * n_rows, (k + 1) * n_rows)
            total = None
            for h in range(2):
                value = a_buf[h, dy, dx]
                hi, lo = split(value * -2.0)
                r_cat[rows, h * half_feat:(h + 1) * half_feat] = hi
                r_cat[rows, n_feat + h * half_feat:n_feat + (h + 1) * half_feat] = hi
                r_cat[rows, 2 * n_feat + h * half_feat:2 * n_feat + (h + 1) * half_feat] = lo
                square = value * value
                total = square if total is None else total + square
            r_norm[rows, :] = jnp.broadcast_to(jnp.sum(total, axis=1, keepdims=True), (n_rows, 128))

    a_round(0)
    ring = {1: b_send(0, 1, right), 7: b_send(0, 7, left)}
    across = {0: b_sibling(0)}
    prepare([(0, 0)])
    a_wait((1, 0), (3, 0), (0, 1), (0, 3))
    a_round(1)
    forward(1)
    prepare([(1, 0), (3, 0), (0, 1), (0, 3)])
    a_wait((2, 0), (1, 1), (1, 3), (3, 1), (3, 3))
    a_round(2)
    forward(2)
    a_wait((0, 2))
    prepare([(1, 1), (1, 3), (3, 1), (3, 3), (2, 0), (0, 2)])
    a_wait((2, 1), (2, 3))
    a_round(3)
    forward(3)
    a_wait((1, 2), (3, 2), (2, 2))
    prepare([(2, 1), (2, 3), (1, 2), (3, 2), (2, 2)])

    def my_rows(c):
        return pl.ds(pl.multiple_of(c * half_rank + here * chunk, chunk), chunk)

    position = lax.broadcasted_iota(jnp.int32, (8, PLANE * n_rows), 1)
    slot = position // n_rows
    from_x = (x + NX - slot % NX) % NX
    from_y = (y + NY - slot // NX) % NY
    point = (((z % ZLO * NY + from_y) * NC + core) * (NX * NZ // ZLO) + z // ZLO * NX + from_x) * n_rows
    point = point + position % n_rows
    onehot = []
    for c in range(NC):
        wanted = pivots_ref[my_rows(c), :]
        onehot.append((point == jnp.concatenate([wanted] * (PLANE * n_rows // 128), axis=1)).astype(f32))
    onehot = jnp.concatenate(onehot, axis=0)
    for h in range(2):
        value = dot_exact(onehot, a_buf[h].reshape(PLANE * n_rows, half_feat))
        pick[:, :, h * half_feat:(h + 1) * half_feat] = value.reshape(NC, chunk, half_feat)

    def line_reduce(src, dst, sem):
        copies = []
        for dz, dc in line_offsets:
            device, cc = line(dz, dc)
            k = dz * NC + dc
            copies.append(send(src.at[cc], dst.at[k], sem, k, device))
        return copies

    def plane_gather(ref, sem):
        copies = []
        for dx, dy in plane_offsets:
            mine = ref.at[my_rows(core)]
            copies.append(send(mine, mine, sem, LINE + dy * NX + dx, plane(dx, dy)[0]))
        return copies

    def sibling_gather(ref, sem):
        mine = ref.at[pl.ds(pl.multiple_of(core * half_rank, half_rank), half_rank)]
        return send(mine, mine, sem, LINE + PLANE, sibling)

    def summed(total, buf, count):
        for k in range(1, count):
            total = total + buf[k]
        return total

    p_line = line_reduce(pick, p_buf, p_sem)

    for k in range(0, r_norm.shape[0], 128):
        r_norm_row[:, k:k + 128] = as_row(r_norm[k:k + 128, :])
    part[...] = jnp.zeros_like(part)
    tile = 256

    def columns(slots):
        for i, (dz, dc) in enumerate(slots):
            rows = slice(i * n_rows, (i + 1) * n_rows)
            value = b_buf[dz * NC + dc, :, :n_feat]
            hi, lo = split(value)
            c_cat[rows, :n_feat] = hi
            c_cat[rows, n_feat:2 * n_feat] = lo
            c_cat[rows, 2 * n_feat:] = hi
            hi, lo = split(b_buf[dz * NC + dc, :, n_feat:])
            v_cat[rows, :n_probe] = hi
            v_cat[rows, n_probe:] = lo
        for i in range(0, len(slots), 2):
            pair = [column_norms(b_buf[dz * NC + dc, :, :n_feat]) for dz, dc in slots[i:i + 2]]
            c_norm_row[:, i * n_rows:(i + 2) * n_rows] = as_row(jnp.concatenate(pair, axis=0))

        def body(i, carry):
            rows = pl.ds(pl.multiple_of(i * tile, tile), tile)
            s = dot_nt(r_cat[rows, :], c_cat[...])
            k = matern(s + twice(r_norm[rows, :]) + c_norm_row[...])
            hi, lo = split(k)
            both = dot_nn(hi, v_cat[...])
            last = dot_nn(lo, v_cat[:, :n_probe])
            part[rows, :] = part[rows, :] + (both[:, :n_probe] + both[:, n_probe:] + last)
            return carry

        lax.fori_loop(0, part.shape[0] // tile, body, 0)

    across[0].wait_recv()
    across[1].wait_recv()
    columns([(0, 0), (0, 1), (1, 0), (1, 1)])

    landed(p_line)
    piv[my_rows(core), :] = summed(pick[core], p_buf, LINE)
    p_plane = plane_gather(piv, p_sem)
    ring[4].wait_recv()
    ring["4b"].wait_recv()
    across[4] = b_sibling(4)

    across[2].wait_recv()
    across[7].wait_recv()
    columns([(7, 0), (7, 1), (2, 0), (2, 1)])

    landed(p_plane)
    p_side = sibling_gather(piv, p_sem)
    across[6].wait_recv()
    across[3].wait_recv()
    columns([(6, 0), (6, 1), (3, 0), (3, 1)])

    p_side.wait_recv()
    pv = piv[...]
    hi, lo = split(pv)
    piv_cat[:, :n_feat] = hi
    piv_cat[:, n_feat:2 * n_feat] = lo
    piv_cat[:, 2 * n_feat:] = hi
    piv_norm = column_norms(pv)
    piv_norm_row = jnp.concatenate([as_row(piv_norm[k:k + 128]) for k in range(0, rank, 128)], axis=1)
    for i in range(r_cat.shape[0] // tile):
        rows = slice(i * tile, (i + 1) * tile)
        s = dot_nt(piv_cat[...], r_cat[rows, :])
        value = amp * matern(s + twice(piv_norm) + r_norm_row[:, rows])
        ct[:, rows] = value
        hi, lo = split(value)
        ct_hi[:, rows] = hi
        ct_lo[:, rows] = lo
    hi, lo = split(jnp.concatenate([ct[my_rows(c), :] for c in range(NC)], axis=0))
    both = dot_nt(jnp.concatenate([hi, lo], axis=0), ct_hi[...])
    g = both[:NC * chunk] + both[NC * chunk:] + dot_nt(hi, ct_lo[...])
    g_src[...] = g.reshape(NC, chunk, rank)
    g_line = line_reduce(g_src, g_buf, g_sem)

    s = dot_nt(r_cat[:n_rows, :], piv_cat[...])
    cross_own[...] = amp * matern(s + twice(r_norm[:n_rows, :]) + piv_norm_row)
    across[5].wait_recv()
    across[4].wait_recv()
    columns([(5, 0), (5, 1), (4, 0), (4, 1)])

    landed(g_line)
    gram[my_rows(core), :] = summed(g_src[core], g_buf, LINE)
    g_plane = plane_gather(gram, g_sem)

    part[...] = part[...] * amp
    part[:n_rows, :] = part[:n_rows, :] + noise * probes_ref[...]
    hi, lo = split(part[...])
    both = dot_nn(ct_hi[...], jnp.concatenate([hi, lo], axis=1))
    q = both[:, :n_probe] + both[:, n_probe:] + dot_nn(ct_lo[...], hi)
    q_all[...] = q.reshape(NC, PLANE, chunk, n_probe)
    q1 = []
    for dx, dy in plane_offsets:
        device, there = plane(dx, dy)
        k = dy * NX + dx
        q1.append(send(q_all.at[:, there], q1_buf.at[k], q1_sem, k, device))

    landed(g_plane)
    g_side = sibling_gather(gram, g_sem)
    r_copies = []
    for dx, dy in plane_offsets:
        k = dy * NX + dx
        source = part.at[pl.ds(k * n_rows, n_rows)]
        r_copies.append(send(source, prod_buf.at[k], r_sem, k, plane(-dx, -dy)[0]))

    hi, lo = split(pv * -2.0)
    s = dot_nt(jnp.concatenate([hi, hi, lo], axis=1), piv_cat[...])
    inner = (noise * amp) * matern(s + twice(piv_norm) + piv_norm_row)
    g_side.wait_recv()
    full[...] = gram[...] + inner

    half = rank // 2
    tiles = half // 8
    work[...] = full[:half, :half].reshape(tiles, 8, half)
    invert(work, 0, tiles // 2)
    landed(q1)
    q_src[...] = summed(q_all[:, here], q1_buf, PLANE)
    q_line = line_reduce(q_src, q_buf, q_sem)
    invert(work, tiles // 2, tiles)
    landed(q_line)
    q_out[my_rows(core), :] = summed(q_src[core], q_buf, LINE)
    q_plane = plane_gather(q_out, q_sem)
    upper_inverse = work[...].reshape(half, half)
    lower = full[half:, :half]
    carried = dot_exact(upper_inverse, full[:half, half:])
    work[...] = (full[half:, half:] - dot_exact(lower, carried)).reshape(tiles, 8, half)
    invert(work, 0, tiles // 2)
    landed(q_plane)
    q_side = sibling_gather(q_out, q_sem)
    invert(work, tiles // 2, tiles)
    q_side.wait_recv()
    lower_inverse = work[...].reshape(half, half)

    def solved(right_side):
        top = dot_exact(upper_inverse, right_side[:half])
        below = dot_exact(lower_inverse, right_side[half:] - dot_exact(lower, top))
        return jnp.concatenate([top - dot_exact(carried, below), below], axis=0)

    projected = q_out[...]
    coefficients = solved(projected)
    coefficients = coefficients + solved(projected - dot_exact(full[...], coefficients))
    landed(r_copies)
    product = summed(part[:n_rows, :], prod_buf, PLANE)
    product_ref[...] = product
    removed = dot_exact(cross_own[...], coefficients)
    out_ref[...] = (product - removed) / noise

    for c in everything:
        c.wait_send()


def per_device(features, probes, outputscale, noise, pivots):
    n_rows, n_feat = features.shape
    n_probe = probes.shape[1]
    rank = pivots.shape[0]
    chunk = rank // NC // PLANE
    wide = PLANE * n_rows
    block = 4 * n_rows
    vmem = pltpu.VMEM
    dma = pltpu.SemaphoreType.DMA
    spread = jnp.broadcast_to(pivots[:, None], (rank, 128))
    return pl.pallas_call(
        exchange_kernel,
        out_shape=(jax.ShapeDtypeStruct((n_rows, n_probe), f32),) * 2,
        in_specs=[pl.BlockSpec(memory_space=vmem)] * 3
        + [pl.BlockSpec(memory_space=pltpu.SMEM)] * 2,
        out_specs=[pl.BlockSpec(memory_space=vmem)] * 2,
        scratch_shapes=[
            vmem((2, NY, NX, n_rows, n_feat // 2), f32),
            vmem((LINE, n_rows, n_feat + n_probe), f32),
            vmem((NC, chunk, n_feat), f32),
            vmem((LINE, chunk, n_feat), f32),
            vmem((rank, n_feat), f32),
            vmem((wide, 3 * n_feat), bf16),
            vmem((wide, 128), f32),
            vmem((1, wide), f32),
            vmem((block, 3 * n_feat), bf16),
            vmem((1, block), f32),
            vmem((block, 2 * n_probe), bf16),
            vmem((wide, n_probe), f32),
            vmem((rank, 3 * n_feat), bf16),
            vmem((rank, wide), f32),
            vmem((rank, wide), bf16),
            vmem((rank, wide), bf16),
            vmem((n_rows, rank), f32),
            vmem((NC, chunk, rank), f32),
            vmem((LINE, chunk, rank), f32),
            vmem((rank, rank), f32),
            vmem((NC, PLANE, chunk, n_probe), f32),
            vmem((PLANE, NC, chunk, n_probe), f32),
            vmem((NC, chunk, n_probe), f32),
            vmem((LINE, chunk, n_probe), f32),
            vmem((rank, n_probe), f32),
            vmem((PLANE, n_rows, n_probe), f32),
            vmem((rank // 16, 8, rank // 2), f32),
            vmem((rank, rank), f32),
            dma((2, 4 * PLANE)),
            dma((2, LINE + 1)),
            dma((2, LINE + PLANE + 1)),
            dma((2, LINE + PLANE + 1)),
            dma((2, LINE + PLANE + 1)),
            dma((2, PLANE)),
            dma((2, PLANE)),
        ],
        compiler_params=pltpu.CompilerParams(
            collective_id=0, has_side_effects=True, vmem_limit_bytes=40 * 1024 * 1024
        ),
        name="exchange",
    )(features, probes, spread, outputscale, noise)


def solution(mesh):
    in_specs = (P(("blk", "row"), None), P(("blk", "row"), None), P(), P(), P())
    out_specs = (P(("blk", "row"), None), P(("blk", "row"), None))
    return jax.shard_map(
        per_device, mesh=mesh, in_specs=in_specs, out_specs=out_specs, check_vma=False
    )
```

```python
import jax
import jax.numpy as jnp
from jax import lax
from jax.experimental import pallas as pl
from jax.experimental.pallas import tpu as pltpu
from jax.sharding import PartitionSpec as P

MESH = pl.DeviceIdType.MESH
highest = lax.Precision.HIGHEST
root_five = 2.23606797749979
f32 = jnp.float32
bf16 = jnp.bfloat16

NX, NY, NZ, NC = 4, 4, 8, 2
ZLO = 4
PLANE = NX * NY
LINE = NZ * NC


def split(x):
    hi = x.astype(bf16)
    return hi, (x - hi.astype(f32)).astype(bf16)


def dot_nt(a, b):
    return lax.dot_general(a, b, (((1,), (1,)), ((), ())), preferred_element_type=f32)


def dot_nn(a, b):
    return jnp.dot(a, b, preferred_element_type=f32)


def matern(scaled_square):
    s = jnp.maximum(scaled_square, 1e-30)
    t = s * lax.rsqrt(s)
    return (1.0 + t + s * (1.0 / 3.0)) * jnp.exp(-t)


def column_norms(x):
    return jnp.broadcast_to(jnp.sum(x * x, axis=1, keepdims=True), (x.shape[0], 128))


def as_row(norms):
    return jnp.transpose(norms)[0:1]


def twice(x):
    return jnp.concatenate([x, x], axis=1)


def dot_exact(a, b):
    return jnp.dot(a, b, precision=highest, preferred_element_type=f32)


def invert(work, between):
    tiles, _, half = work.shape
    sub = lax.broadcasted_iota(jnp.int32, (8, half), 0)
    lane = lax.broadcasted_iota(jnp.int32, (8, half), 1)

    def spread_lane(v, index):
        return jnp.take_along_axis(v, index, axis=1)

    def spread_row(v, r):
        return jnp.broadcast_to(v[r:r + 1, :], v.shape)

    def reciprocal(d):
        r = pl.reciprocal(d, approx=True)
        r = r * (2.0 - d * r)
        return r * (2.0 - d * r)

    def lanes_of(block):
        first = jnp.clip(block, 0, tiles - 1) * 8
        return [jnp.full((8, half), first + c, jnp.int32) for c in range(8)]

    def in_block(block):
        return (lane >= block * 8) & (lane < block * 8 + 8)

    def eliminated(d, top, block):
        d = list(d)
        top = jnp.where(in_block(block), jnp.where(lane - block * 8 == sub, 1.0, 0.0), top)
        for s in range(0, 8, 2):
            a, b, c = spread_row(d[s], s), spread_row(d[s + 1], s), spread_row(d[s + 1], s + 1)
            inverse = reciprocal(a * c - b * b)
            a, b, c = a * inverse, b * inverse, c * inverse
            first, second = d[s], d[s + 1]

            def swept(v):
                r0, r1 = spread_row(v, s), spread_row(v, s + 1)
                p0 = c * r0 - b * r1
                p1 = a * r1 - b * r0
                rest = v - first * p0 - second * p1
                return jnp.where(sub == s, p0, jnp.where(sub == s + 1, p1, rest))

            for c2 in range(s + 2, 8):
                d[c2] = swept(d[c2])
            top = swept(top)
        return top

    def updated(v, mask, index, rows):
        total = jnp.where(mask, 0.0, v)
        for c in range(8):
            total = total - spread_lane(v, index[c]) * rows[c]
        return total

    def step(block, carry):
        d, top, last = carry
        done = eliminated(d, top, block)
        mask, index = in_block(block - 1), lanes_of(block - 1)
        rows = [spread_row(last, c) for c in range(8)]
        for r in range(tiles):
            work[r] = updated(work[r], mask, index, rows)
        work[jnp.maximum(block - 1, 0)] = last
        v = work[jnp.minimum(block + 1, tiles - 1)]
        top = updated(v, in_block(block), lanes_of(block), [spread_row(done, c) for c in range(8)])
        index = lanes_of(block + 1)
        return tuple(spread_lane(top, index[c]) for c in range(8)), top, done

    top = work[0]
    index = lanes_of(0)
    carry = (tuple(spread_lane(top, index[c]) for c in range(8)), top, jnp.zeros_like(top))
    carry = lax.fori_loop(0, tiles // 2, step, carry)
    between()
    lax.fori_loop(tiles // 2, tiles + 1, step, carry)


def exchange_kernel(
    feats_ref, probes_ref, pivots_ref, amp_ref, noise_ref,
    product_ref, out_ref,
    a_buf, b_buf, pick, p1_buf, p_src, p_buf, piv,
    r_cat, r_norm, r_norm_row, c_cat, c_norm_row, v_cat, part,
    piv_cat, ct, ct_hi, ct_lo, cross_own, g_src, g_buf, gram, q_all, q1_buf, q_src, q_buf, q_out, prod_buf, work, full,
    a_sem, b_sem, p_sem, g_sem, q_sem, p1_sem, q1_sem, r_sem,
):
    n_rows, n_feat = feats_ref.shape
    n_probe = probes_ref.shape[1]
    rank = pivots_ref.shape[0]
    half_rank = rank // NC
    chunk = half_rank // PLANE
    half_feat = n_feat // 2
    blk, row = lax.axis_index("blk"), lax.axis_index("row")
    core = lax.rem(blk, NC)
    y = lax.rem(lax.div(blk, NC), NY)
    x = lax.rem(row, NX)
    z = lax.div(row, NX) * ZLO + lax.div(blk, NC * NY)
    here = y * NX + x

    def plane(dx, dy):
        xx, yy = lax.rem(x + (dx + NX), NX), lax.rem(y + (dy + NY), NY)
        return ((lax.div(blk, NC * NY) * NY + yy) * NC + core, lax.div(row, NX) * NX + xx), yy * NX + xx

    def line(dz, dc):
        zz, cc = lax.rem(z + (dz + NZ), NZ), lax.rem(core + dc, NC)
        return ((lax.rem(zz, ZLO) * NY + y) * NC + cc, lax.div(zz, ZLO) * NX + x), cc

    plane_offsets = sorted(
        [(dx, dy) for dx in range(NX) for dy in range(NY) if dx or dy],
        key=lambda o: -(min(o[0], NX - o[0]) + min(o[1], NY - o[1])),
    )
    line_offsets = sorted(
        [(dz, dc) for dz in range(NZ) for dc in range(NC) if dz or dc],
        key=lambda o: -min(o[0], NZ - o[0]),
    )

    everything = []

    def send(src, dst, sem, k, device):
        copy = pltpu.make_async_remote_copy(
            src_ref=src, dst_ref=dst, send_sem=sem.at[0, k], recv_sem=sem.at[1, k],
            device_id=device, device_id_type=MESH,
        )
        copy.start()
        everything.append(copy)
        return copy

    barrier = pltpu.get_barrier_semaphore()
    for dx, dy in plane_offsets:
        pl.semaphore_signal(barrier, inc=1, device_id=plane(dx, dy)[0], device_id_type=MESH)
    for dz, dc in line_offsets:
        pl.semaphore_signal(barrier, inc=1, device_id=line(dz, dc)[0], device_id_type=MESH)

    amp, noise = amp_ref[0], noise_ref[0]
    own = feats_ref[...] * root_five
    a_buf[0, 0, 0] = own[:, :half_feat]
    a_buf[1, 0, 0] = own[:, half_feat:]
    b_buf[0, :, :n_feat] = own
    b_buf[0, :, n_feat:] = probes_ref[...]
    first = (blk * (NX * NZ // ZLO) + row) * n_rows
    point = lax.broadcasted_iota(jnp.int32, (rank, n_rows), 1) + first
    onehot = (point == pivots_ref[:, :n_rows]).astype(f32)
    pick[...] = dot_exact(onehot, own).reshape(NC, PLANE, chunk, n_feat)
    pl.semaphore_wait(barrier, PLANE + LINE - 2)

    def landed(copies):
        for c in copies:
            c.wait_recv()

    upper_rows, lower_rows = pl.ds(0, n_rows // 2), pl.ds(n_rows // 2, n_rows // 2)

    moved = {}

    def a_slot(h, u, v):
        return a_buf.at[(h, v, u) if h == 0 else (h, u, v)]

    def a_send(h, u, v, du, dv):
        to = ((u + du) % 4, (v + dv) % 4)
        device = plane(du, dv)[0] if h == 0 else plane(dv, du)[0]
        moved[(h, *to)] = send(a_slot(h, u, v), a_slot(h, *to), a_sem, 16 * h + 4 * to[0] + to[1], device)

    def a_wait(*slots):
        for u, v in slots:
            for h in range(2):
                moved[(h, u, v)].wait_recv()

    def a_start():
        for d in (1, -1, 2):
            for h in range(2):
                a_send(h, 0, 0, d, 0)
                a_send(h, 0, 0, 0, d)

    def a_forward(*steps):
        for d in (1, -1, 2):
            for h in range(2):
                for u in steps:
                    a_send(h, u, 0, 0, d)

    right, left = line(1, 0)[0], line(-1, 0)[0]
    sibling = line(0, 1)[0]

    def b_slot(dz, dc):
        return b_buf.at[dz * NC + dc]

    def b_send(dz_from, dz_to, device):
        return send(b_slot(dz_from, 0), b_slot(dz_to, 0), b_sem, dz_to * NC, device)

    def b_sibling(dz):
        return send(b_slot(dz, 0), b_slot(dz, 1), b_sem, dz * NC + 1, sibling)

    def forward(step):
        ring[step].wait_recv()
        ring[8 - step].wait_recv()
        if step < 3:
            ring[step + 1] = b_send(step, step + 1, right)
            ring[7 - step] = b_send(8 - step, 7 - step, left)
        else:
            ring[4] = send(b_slot(3, 0).at[upper_rows], b_slot(4, 0).at[upper_rows], b_sem, 8, right)
            ring["4b"] = send(b_slot(5, 0).at[lower_rows], b_slot(4, 0).at[lower_rows], b_sem, LINE, left)
        across[step] = b_sibling(step)
        across[8 - step] = b_sibling(8 - step)

    def prepare(slots):
        for dx, dy in slots:
            k = dy * NX + dx
            rows = slice(k * n_rows, (k + 1) * n_rows)
            total = None
            for h in range(2):
                value = a_buf[h, dy, dx]
                hi, lo = split(value * -2.0)
                r_cat[rows, h * half_feat:(h + 1) * half_feat] = hi
                r_cat[rows, n_feat + h * half_feat:n_feat + (h + 1) * half_feat] = hi
                r_cat[rows, 2 * n_feat + h * half_feat:2 * n_feat + (h + 1) * half_feat] = lo
                square = value * value
                total = square if total is None else total + square
            r_norm[rows, :] = jnp.broadcast_to(jnp.sum(total, axis=1, keepdims=True), (n_rows, 128))

    def my_rows(c):
        return pl.ds(pl.multiple_of(c * half_rank + here * chunk, chunk), chunk)

    def line_reduce(src, dst, sem):
        copies = []
        for dz, dc in line_offsets:
            device, cc = line(dz, dc)
            k = dz * NC + dc
            copies.append(send(src.at[cc], dst.at[k], sem, k, device))
        return copies

    def plane_gather(ref, sem):
        copies = []
        mine = ref.at[my_rows(core)]
        for dx, dy in plane_offsets:
            k = LINE + dy * NX + dx
            (other_blk, other_row), _ = plane(dx, dy)
            copies.append(send(mine, mine, sem, k, (other_blk, other_row)))
            copies.append(send(mine, mine, sem, k + PLANE, (other_blk + 1 - 2 * core, other_row)))
        copies.append(send(mine, mine, sem, LINE + PLANE, sibling))
        return copies

    def plane_scatter(src, dst, sem):
        copies = []
        for dx, dy in plane_offsets:
            device, there = plane(dx, dy)
            k = dy * NX + dx
            copies.append(send(src.at[:, there], dst.at[k], sem, k, device))
        return copies

    def summed(total, buf, count):
        for k in range(1, count):
            total = total + buf[k]
        return total

    p_scatter = plane_scatter(pick, p1_buf, p1_sem)
    a_start()
    ring = {1: b_send(0, 1, right), 7: b_send(0, 7, left)}
    across = {0: b_sibling(0)}
    prepare([(0, 0)])
    a_wait((1, 0), (3, 0))
    a_forward(1, 3)
    a_wait((2, 0))
    a_forward(2)
    landed(p_scatter)
    p_src[...] = summed(pick[:, here], p1_buf, PLANE)
    p_line = line_reduce(p_src, p_buf, p_sem)
    forward(1)
    a_wait((0, 1), (0, 3), (0, 2))
    prepare([(1, 0), (3, 0), (2, 0), (0, 1), (0, 3), (0, 2)])
    a_wait((1, 1), (1, 3), (3, 1), (3, 3), (1, 2), (3, 2), (2, 1), (2, 3), (2, 2))
    prepare([(1, 1), (1, 3), (3, 1), (3, 3), (2, 1), (2, 3), (1, 2), (3, 2), (2, 2)])

    landed(p_line)
    piv[my_rows(core), :] = summed(p_src[core], p_buf, LINE)
    p_plane = plane_gather(piv, p_sem)
    forward(2)

    for k in range(0, r_norm.shape[0], 128):
        r_norm_row[:, k:k + 128] = as_row(r_norm[k:k + 128, :])
    part[...] = jnp.zeros_like(part)
    tile = 256

    def columns(slots):
        for i, (dz, dc) in enumerate(slots):
            rows = slice(i * n_rows, (i + 1) * n_rows)
            value = b_buf[dz * NC + dc, :, :n_feat]
            hi, lo = split(value)
            c_cat[rows, :n_feat] = hi
            c_cat[rows, n_feat:2 * n_feat] = lo
            c_cat[rows, 2 * n_feat:] = hi
            hi, lo = split(b_buf[dz * NC + dc, :, n_feat:])
            v_cat[rows, :n_probe] = hi
            v_cat[rows, n_probe:] = lo
        for i in range(0, len(slots), 2):
            pair = [column_norms(b_buf[dz * NC + dc, :, :n_feat]) for dz, dc in slots[i:i + 2]]
            c_norm_row[:, i * n_rows:(i + 2) * n_rows] = as_row(jnp.concatenate(pair, axis=0))

        def body(i, carry):
            rows = pl.ds(pl.multiple_of(i * tile, tile), tile)
            s = dot_nt(r_cat[rows, :], c_cat[...])
            k = matern(s + twice(r_norm[rows, :]) + c_norm_row[...])
            hi, lo = split(k)
            both = dot_nn(hi, v_cat[...])
            last = dot_nn(lo, v_cat[:, :n_probe])
            part[rows, :] = part[rows, :] + (both[:, :n_probe] + both[:, n_probe:] + last)
            return carry

        lax.fori_loop(0, part.shape[0] // tile, body, 0)

    across[0].wait_recv()
    across[1].wait_recv()
    columns([(0, 0), (0, 1), (1, 0), (1, 1)])

    landed(p_plane)
    pv = piv[...]
    hi, lo = split(pv)
    piv_cat[:, :n_feat] = hi
    piv_cat[:, n_feat:2 * n_feat] = lo
    piv_cat[:, 2 * n_feat:] = hi
    piv_norm = column_norms(pv)
    piv_norm_row = jnp.concatenate([as_row(piv_norm[k:k + 128]) for k in range(0, rank, 128)], axis=1)
    for i in range(r_cat.shape[0] // tile):
        rows = slice(i * tile, (i + 1) * tile)
        s = dot_nt(piv_cat[...], r_cat[rows, :])
        value = amp * matern(s + twice(piv_norm) + r_norm_row[:, rows])
        ct[:, rows] = value
        hi, lo = split(value)
        ct_hi[:, rows] = hi
        ct_lo[:, rows] = lo
    hi, lo = split(jnp.concatenate([ct[my_rows(c), :] for c in range(NC)], axis=0))
    both = dot_nt(jnp.concatenate([hi, lo], axis=0), ct_hi[...])
    g = both[:NC * chunk] + both[NC * chunk:] + dot_nt(hi, ct_lo[...])
    g_src[...] = g.reshape(NC, chunk, rank)
    g_line = line_reduce(g_src, g_buf, g_sem)

    s = dot_nt(r_cat[:n_rows, :], piv_cat[...])
    cross_own[...] = amp * matern(s + twice(r_norm[:n_rows, :]) + piv_norm_row)
    forward(3)
    across[2].wait_recv()
    across[7].wait_recv()
    columns([(7, 0), (7, 1), (2, 0), (2, 1)])
    across[6].wait_recv()
    across[3].wait_recv()
    columns([(6, 0), (6, 1), (3, 0), (3, 1)])

    landed(g_line)
    gram[my_rows(core), :] = summed(g_src[core], g_buf, LINE)
    g_plane = plane_gather(gram, g_sem)
    ring[4].wait_recv()
    ring["4b"].wait_recv()
    across[4] = b_sibling(4)
    hi, lo = split(pv * -2.0)
    s = dot_nt(jnp.concatenate([hi, hi, lo], axis=1), piv_cat[...])
    full[...] = (noise * amp) * matern(s + twice(piv_norm) + piv_norm_row)
    across[5].wait_recv()
    across[4].wait_recv()
    columns([(5, 0), (5, 1), (4, 0), (4, 1)])

    part[...] = part[...] * amp
    part[:n_rows, :] = part[:n_rows, :] + noise * probes_ref[...]
    hi, lo = split(part[...])
    both = dot_nn(ct_hi[...], jnp.concatenate([hi, lo], axis=1))
    q = both[:, :n_probe] + both[:, n_probe:] + dot_nn(ct_lo[...], hi)
    q_all[...] = q.reshape(NC, PLANE, chunk, n_probe)
    q1 = plane_scatter(q_all, q1_buf, q1_sem)
    landed(g_plane)
    r_copies = []
    for dx, dy in plane_offsets:
        k = dy * NX + dx
        source = part.at[pl.ds(k * n_rows, n_rows)]
        r_copies.append(send(source, prod_buf.at[k], r_sem, k, plane(-dx, -dy)[0]))
    full[...] = full[...] + gram[...]

    half = rank // 2
    tiles = half // 8
    work[...] = full[:half, :half].reshape(tiles, 8, half)
    sent = {}

    def reduce_projected():
        landed(q1)
        q_src[...] = summed(q_all[:, here], q1_buf, PLANE)
        sent["line"] = line_reduce(q_src, q_buf, q_sem)

    def gather_projected():
        landed(sent["line"])
        q_out[my_rows(core), :] = summed(q_src[core], q_buf, LINE)
        sent["plane"] = plane_gather(q_out, q_sem)

    invert(work, reduce_projected)
    upper_inverse = work[...].reshape(half, half)
    lower = full[half:, :half]
    carried = dot_exact(upper_inverse, full[:half, half:])
    work[...] = (full[half:, half:] - dot_exact(lower, carried)).reshape(tiles, 8, half)
    invert(work, gather_projected)
    landed(sent["plane"])
    lower_inverse = work[...].reshape(half, half)

    def solved(right_side):
        top = dot_exact(upper_inverse, right_side[:half])
        below = dot_exact(lower_inverse, right_side[half:] - dot_exact(lower, top))
        return jnp.concatenate([top - dot_exact(carried, below), below], axis=0)

    projected = q_out[...]
    coefficients = solved(projected)
    coefficients = coefficients + solved(projected - dot_exact(full[...], coefficients))
    landed(r_copies)
    product = summed(part[:n_rows, :], prod_buf, PLANE)
    product_ref[...] = product
    removed = dot_exact(cross_own[...], coefficients)
    out_ref[...] = (product - removed) / noise

    for c in everything:
        c.wait_send()


def per_device(features, probes, outputscale, noise, pivots):
    n_rows, n_feat = features.shape
    n_probe = probes.shape[1]
    rank = pivots.shape[0]
    chunk = rank // NC // PLANE
    wide = PLANE * n_rows
    block = 4 * n_rows
    vmem = pltpu.VMEM
    dma = pltpu.SemaphoreType.DMA
    spread = jnp.broadcast_to(pivots[:, None], (rank, 128))
    return pl.pallas_call(
        exchange_kernel,
        out_shape=(jax.ShapeDtypeStruct((n_rows, n_probe), f32),) * 2,
        in_specs=[pl.BlockSpec(memory_space=vmem)] * 3
        + [pl.BlockSpec(memory_space=pltpu.SMEM)] * 2,
        out_specs=[pl.BlockSpec(memory_space=vmem)] * 2,
        scratch_shapes=[
            vmem((2, NY, NX, n_rows, n_feat // 2), f32),
            vmem((LINE, n_rows, n_feat + n_probe), f32),
            vmem((NC, PLANE, chunk, n_feat), f32),
            vmem((PLANE, NC, chunk, n_feat), f32),
            vmem((NC, chunk, n_feat), f32),
            vmem((LINE, chunk, n_feat), f32),
            vmem((rank, n_feat), f32),
            vmem((wide, 3 * n_feat), bf16),
            vmem((wide, 128), f32),
            vmem((1, wide), f32),
            vmem((block, 3 * n_feat), bf16),
            vmem((1, block), f32),
            vmem((block, 2 * n_probe), bf16),
            vmem((wide, n_probe), f32),
            vmem((rank, 3 * n_feat), bf16),
            vmem((rank, wide), f32),
            vmem((rank, wide), bf16),
            vmem((rank, wide), bf16),
            vmem((n_rows, rank), f32),
            vmem((NC, chunk, rank), f32),
            vmem((LINE, chunk, rank), f32),
            vmem((rank, rank), f32),
            vmem((NC, PLANE, chunk, n_probe), f32),
            vmem((PLANE, NC, chunk, n_probe), f32),
            vmem((NC, chunk, n_probe), f32),
            vmem((LINE, chunk, n_probe), f32),
            vmem((rank, n_probe), f32),
            vmem((PLANE, n_rows, n_probe), f32),
            vmem((rank // 16, 8, rank // 2), f32),
            vmem((rank, rank), f32),
            dma((2, 2 * PLANE)),
            dma((2, LINE + 1)),
            dma((2, LINE + 2 * PLANE)),
            dma((2, LINE + 2 * PLANE)),
            dma((2, LINE + 2 * PLANE)),
            dma((2, PLANE)),
            dma((2, PLANE)),
            dma((2, PLANE)),
        ],
        compiler_params=pltpu.CompilerParams(
            collective_id=0, has_side_effects=True, vmem_limit_bytes=40 * 1024 * 1024
        ),
        name="exchange",
    )(features, probes, spread, outputscale, noise)


def solution(mesh):
    in_specs = (P(("blk", "row"), None), P(("blk", "row"), None), P(), P(), P())
    out_specs = (P(("blk", "row"), None), P(("blk", "row"), None))
    return jax.shard_map(
        per_device, mesh=mesh, in_specs=in_specs, out_specs=out_specs, check_vma=False
    )
```

```python
import jax
import jax.numpy as jnp
from jax import lax
from jax.experimental import pallas as pl
from jax.experimental.pallas import tpu as pltpu
from jax.sharding import PartitionSpec as P

MESH = pl.DeviceIdType.MESH
highest = lax.Precision.HIGHEST
root_five = 2.23606797749979
f32 = jnp.float32
bf16 = jnp.bfloat16

NX, NY, NZ, NC = 4, 4, 8, 2
ZLO = 4
PLANE = NX * NY
LINE = NZ * NC


def split(x):
    hi = x.astype(bf16)
    return hi, (x - hi.astype(f32)).astype(bf16)


def dot_nt(a, b):
    return lax.dot_general(a, b, (((1,), (1,)), ((), ())), preferred_element_type=f32)


def dot_nn(a, b):
    return jnp.dot(a, b, preferred_element_type=f32)


def matern(scaled_square):
    s = jnp.maximum(scaled_square, 1e-30)
    t = s * lax.rsqrt(s)
    return (1.0 + t + s * (1.0 / 3.0)) * jnp.exp(-t)


def column_norms(x):
    return jnp.broadcast_to(jnp.sum(x * x, axis=1, keepdims=True), (x.shape[0], 128))


def as_row(norms):
    return jnp.transpose(norms)[0:1]


def twice(x):
    return jnp.concatenate([x, x], axis=1)


def dot_exact(a, b):
    return jnp.dot(a, b, precision=highest, preferred_element_type=f32)


def invert(work):
    tiles, _, half = work.shape
    sub = lax.broadcasted_iota(jnp.int32, (8, half), 0)
    lane = lax.broadcasted_iota(jnp.int32, (8, half), 1)

    def spread_lane(v, c):
        return jnp.take_along_axis(v, jnp.full((8, half), c, jnp.int32), axis=1)

    def spread_row(v, r):
        return jnp.broadcast_to(v[r:r + 1, :], v.shape)

    def reciprocal(d):
        r = pl.reciprocal(d, approx=True)
        r = r * (2.0 - d * r)
        return r * (2.0 - d * r)

    def in_block(block):
        return (lane >= block * 8) & (lane < block * 8 + 8)

    def eliminated(top, block):
        d = [spread_lane(top, 8 * block + c) for c in range(8)]
        top = jnp.where(in_block(block), jnp.where(lane - block * 8 == sub, 1.0, 0.0), top)
        for s in range(0, 8, 2):
            a, b, c = spread_row(d[s], s), spread_row(d[s + 1], s), spread_row(d[s + 1], s + 1)
            inverse = reciprocal(a * c - b * b)
            first, second = d[s], d[s + 1]

            def swept(v):
                r0, r1 = spread_row(v, s), spread_row(v, s + 1)
                n0 = c * r0 - b * r1
                n1 = a * r1 - b * r0
                taken = jnp.where(sub == s, n0, jnp.where(sub == s + 1, n1, -(first * n0 + second * n1)))
                kept = jnp.where((sub == s) | (sub == s + 1), 0.0, v)
                return kept + taken * inverse

            for c2 in range(s + 2, 8):
                d[c2] = swept(d[c2])
            top = swept(top)
        return top

    def updated(v, block, rows):
        total = jnp.where(in_block(block), 0.0, v)
        for c in range(8):
            total = total - spread_lane(v, 8 * block + c) * rows[c]
        return total

    panel = tiles // 4
    for p in range(0, tiles, panel):
        block_rows = [work[p + i] for i in range(panel)]
        for i in range(panel):
            done = eliminated(block_rows[i], p + i)
            rows = [spread_row(done, c) for c in range(8)]
            for other in range(panel):
                if other != i:
                    block_rows[other] = updated(block_rows[other], p + i, rows)
            block_rows[i] = done
        reduced = jnp.concatenate(block_rows, axis=0)
        whole = work[...].reshape(half, half)
        first, last = 8 * p, 8 * (p + panel)
        column = lax.broadcasted_iota(jnp.int32, (half, half), 1)
        rest = jnp.where((column >= first) & (column < last), 0.0, whole)
        rest = rest - dot_exact(whole[:, first:last], reduced)
        work[...] = rest.reshape(tiles, 8, half)
        for i in range(panel):
            work[p + i] = block_rows[i]


def exchange_kernel(
    feats_ref, probes_ref, pivots_ref, amp_ref, noise_ref,
    product_ref, out_ref,
    a_buf, b_buf, pick, p1_buf, p_src, p_buf, piv,
    r_cat, r_norm, r_norm_row, c_cat, c_norm_row, v_cat, part,
    piv_cat, ct, ct_hi, ct_lo, cross_own, g_src, g_buf, gram, q_all, q1_buf, q_src, q_buf, q_out, prod_buf, work, full,
    a_sem, b_sem, p_sem, g_sem, q_sem, p1_sem, q1_sem, r_sem,
):
    n_rows, n_feat = feats_ref.shape
    n_probe = probes_ref.shape[1]
    rank = pivots_ref.shape[0]
    half_rank = rank // NC
    chunk = half_rank // PLANE
    half_feat = n_feat // 2
    blk, row = lax.axis_index("blk"), lax.axis_index("row")
    core = lax.rem(blk, NC)
    y = lax.rem(lax.div(blk, NC), NY)
    x = lax.rem(row, NX)
    z = lax.div(row, NX) * ZLO + lax.div(blk, NC * NY)
    here = y * NX + x

    def plane(dx, dy):
        xx, yy = lax.rem(x + (dx + NX), NX), lax.rem(y + (dy + NY), NY)
        return ((lax.div(blk, NC * NY) * NY + yy) * NC + core, lax.div(row, NX) * NX + xx), yy * NX + xx

    def line(dz, dc):
        zz, cc = lax.rem(z + (dz + NZ), NZ), lax.rem(core + dc, NC)
        return ((lax.rem(zz, ZLO) * NY + y) * NC + cc, lax.div(zz, ZLO) * NX + x), cc

    plane_offsets = sorted(
        [(dx, dy) for dx in range(NX) for dy in range(NY) if dx or dy],
        key=lambda o: -(min(o[0], NX - o[0]) + min(o[1], NY - o[1])),
    )
    line_offsets = sorted(
        [(dz, dc) for dz in range(NZ) for dc in range(NC) if dz or dc],
        key=lambda o: -min(o[0], NZ - o[0]),
    )

    everything = []

    def send(src, dst, sem, k, device):
        copy = pltpu.make_async_remote_copy(
            src_ref=src, dst_ref=dst, send_sem=sem.at[0, k], recv_sem=sem.at[1, k],
            device_id=device, device_id_type=MESH,
        )
        copy.start()
        everything.append(copy)
        return copy

    barrier = pltpu.get_barrier_semaphore()
    for dx, dy in plane_offsets:
        pl.semaphore_signal(barrier, inc=1, device_id=plane(dx, dy)[0], device_id_type=MESH)
    for dz, dc in line_offsets:
        pl.semaphore_signal(barrier, inc=1, device_id=line(dz, dc)[0], device_id_type=MESH)

    amp, noise = amp_ref[0], noise_ref[0]
    own = feats_ref[...] * root_five
    a_buf[0, 0, 0] = own[:, :half_feat]
    a_buf[1, 0, 0] = own[:, half_feat:]
    b_buf[0, :, :n_feat] = own
    b_buf[0, :, n_feat:] = probes_ref[...]
    first = (blk * (NX * NZ // ZLO) + row) * n_rows
    point = lax.broadcasted_iota(jnp.int32, (rank, n_rows), 1) + first
    onehot = (point == pivots_ref[:, :n_rows]).astype(f32)
    pick[...] = dot_exact(onehot, own).reshape(NC, PLANE, chunk, n_feat)
    pl.semaphore_wait(barrier, PLANE + LINE - 2)

    def landed(copies):
        for c in copies:
            c.wait_recv()

    upper_rows, lower_rows = pl.ds(0, n_rows // 2), pl.ds(n_rows // 2, n_rows // 2)

    moved = {}

    def a_slot(h, u, v):
        return a_buf.at[(h, v, u) if h == 0 else (h, u, v)]

    def a_send(h, u, v, du, dv):
        to = ((u + du) % 4, (v + dv) % 4)
        device = plane(du, dv)[0] if h == 0 else plane(dv, du)[0]
        moved[(h, *to)] = send(a_slot(h, u, v), a_slot(h, *to), a_sem, 16 * h + 4 * to[0] + to[1], device)

    def a_wait(*slots):
        for u, v in slots:
            for h in range(2):
                moved[(h, u, v)].wait_recv()

    def a_start():
        for d in (1, -1, 2):
            for h in range(2):
                a_send(h, 0, 0, d, 0)
                a_send(h, 0, 0, 0, d)

    def a_forward(*steps):
        for d in (1, -1, 2):
            for h in range(2):
                for u in steps:
                    a_send(h, u, 0, 0, d)

    right, left = line(1, 0)[0], line(-1, 0)[0]
    sibling = line(0, 1)[0]

    def b_slot(dz, dc):
        return b_buf.at[dz * NC + dc]

    def b_send(dz_from, dz_to, device):
        return send(b_slot(dz_from, 0), b_slot(dz_to, 0), b_sem, dz_to * NC, device)

    def b_sibling(dz):
        return send(b_slot(dz, 0), b_slot(dz, 1), b_sem, dz * NC + 1, sibling)

    def forward(step):
        ring[step].wait_recv()
        ring[8 - step].wait_recv()
        if step < 3:
            ring[step + 1] = b_send(step, step + 1, right)
            ring[7 - step] = b_send(8 - step, 7 - step, left)
        else:
            ring[4] = send(b_slot(3, 0).at[upper_rows], b_slot(4, 0).at[upper_rows], b_sem, 8, right)
            ring["4b"] = send(b_slot(5, 0).at[lower_rows], b_slot(4, 0).at[lower_rows], b_sem, LINE, left)
        across[step] = b_sibling(step)
        across[8 - step] = b_sibling(8 - step)

    def prepare(slots):
        for dx, dy in slots:
            k = dy * NX + dx
            rows = slice(k * n_rows, (k + 1) * n_rows)
            total = None
            for h in range(2):
                value = a_buf[h, dy, dx]
                hi, lo = split(value * -2.0)
                r_cat[rows, h * half_feat:(h + 1) * half_feat] = hi
                r_cat[rows, n_feat + h * half_feat:n_feat + (h + 1) * half_feat] = hi
                r_cat[rows, 2 * n_feat + h * half_feat:2 * n_feat + (h + 1) * half_feat] = lo
                square = value * value
                total = square if total is None else total + square
            r_norm[rows, :] = jnp.broadcast_to(jnp.sum(total, axis=1, keepdims=True), (n_rows, 128))

    def my_rows(c):
        return pl.ds(pl.multiple_of(c * half_rank + here * chunk, chunk), chunk)

    def line_reduce(src, dst, sem):
        copies = []
        for dz, dc in line_offsets:
            device, cc = line(dz, dc)
            k = dz * NC + dc
            copies.append(send(src.at[cc], dst.at[k], sem, k, device))
        return copies

    def plane_gather(ref, sem):
        copies = []
        mine = ref.at[my_rows(core)]
        for dx, dy in plane_offsets:
            k = LINE + dy * NX + dx
            (other_blk, other_row), _ = plane(dx, dy)
            copies.append(send(mine, mine, sem, k, (other_blk, other_row)))
            copies.append(send(mine, mine, sem, k + PLANE, (other_blk + 1 - 2 * core, other_row)))
        copies.append(send(mine, mine, sem, LINE + PLANE, sibling))
        return copies

    def plane_scatter(src, dst, sem):
        copies = []
        for dx, dy in plane_offsets:
            device, there = plane(dx, dy)
            k = dy * NX + dx
            copies.append(send(src.at[:, there], dst.at[k], sem, k, device))
        return copies

    def summed(total, buf, count):
        for k in range(1, count):
            total = total + buf[k]
        return total

    p_scatter = plane_scatter(pick, p1_buf, p1_sem)
    ring = {1: b_send(0, 1, right), 7: b_send(0, 7, left)}
    across = {0: b_sibling(0)}
    a_start()
    prepare([(0, 0)])
    a_wait((1, 0), (3, 0))
    a_forward(1, 3)
    forward(1)
    a_wait((2, 0))
    a_forward(2)
    landed(p_scatter)
    p_src[...] = summed(pick[:, here], p1_buf, PLANE)
    p_line = line_reduce(p_src, p_buf, p_sem)
    a_wait((0, 1), (0, 3), (0, 2))
    prepare([(1, 0), (3, 0), (2, 0), (0, 1), (0, 3), (0, 2)])
    forward(2)
    landed(p_line)
    piv[my_rows(core), :] = summed(p_src[core], p_buf, LINE)
    p_plane = plane_gather(piv, p_sem)
    a_wait((1, 1), (1, 3), (3, 1), (3, 3), (1, 2), (3, 2), (2, 1), (2, 3), (2, 2))
    prepare([(1, 1), (1, 3), (3, 1), (3, 3), (2, 1), (2, 3), (1, 2), (3, 2), (2, 2)])
    forward(3)

    for k in range(0, r_norm.shape[0], 128):
        r_norm_row[:, k:k + 128] = as_row(r_norm[k:k + 128, :])
    part[...] = jnp.zeros_like(part)
    tile = 256

    def columns(slots):
        for i, (dz, dc) in enumerate(slots):
            rows = slice(i * n_rows, (i + 1) * n_rows)
            value = b_buf[dz * NC + dc, :, :n_feat]
            hi, lo = split(value)
            c_cat[rows, :n_feat] = hi
            c_cat[rows, n_feat:2 * n_feat] = lo
            c_cat[rows, 2 * n_feat:] = hi
            hi, lo = split(b_buf[dz * NC + dc, :, n_feat:])
            v_cat[rows, :n_probe] = hi
            v_cat[rows, n_probe:] = lo
        for i in range(0, len(slots), 2):
            pair = [column_norms(b_buf[dz * NC + dc, :, :n_feat]) for dz, dc in slots[i:i + 2]]
            c_norm_row[:, i * n_rows:(i + 2) * n_rows] = as_row(jnp.concatenate(pair, axis=0))

        def body(i, carry):
            rows = pl.ds(pl.multiple_of(i * tile, tile), tile)
            s = dot_nt(r_cat[rows, :], c_cat[...])
            k = matern(s + twice(r_norm[rows, :]) + c_norm_row[...])
            hi, lo = split(k)
            both = dot_nn(hi, v_cat[...])
            last = dot_nn(lo, v_cat[:, :n_probe])
            part[rows, :] = part[rows, :] + (both[:, :n_probe] + both[:, n_probe:] + last)
            return carry

        lax.fori_loop(0, part.shape[0] // tile, body, 0, unroll=2)

    across[0].wait_recv()
    across[1].wait_recv()
    columns([(0, 0), (0, 1), (1, 0), (1, 1)])

    across[2].wait_recv()
    across[7].wait_recv()
    columns([(7, 0), (7, 1), (2, 0), (2, 1)])
    landed(p_plane)
    pv = piv[...]
    hi, lo = split(pv)
    piv_cat[:, :n_feat] = hi
    piv_cat[:, n_feat:2 * n_feat] = lo
    piv_cat[:, 2 * n_feat:] = hi
    piv_norm = column_norms(pv)
    piv_norm_row = jnp.concatenate([as_row(piv_norm[k:k + 128]) for k in range(0, rank, 128)], axis=1)
    for i in range(r_cat.shape[0] // tile):
        rows = slice(i * tile, (i + 1) * tile)
        s = dot_nt(piv_cat[...], r_cat[rows, :])
        value = amp * matern(s + twice(piv_norm) + r_norm_row[:, rows])
        ct[:, rows] = value
        hi, lo = split(value)
        ct_hi[:, rows] = hi
        ct_lo[:, rows] = lo
    hi, lo = split(jnp.concatenate([ct[my_rows(c), :] for c in range(NC)], axis=0))
    both = dot_nt(jnp.concatenate([hi, lo], axis=0), ct_hi[...])
    g = both[:NC * chunk] + both[NC * chunk:] + dot_nt(hi, ct_lo[...])
    g_src[...] = g.reshape(NC, chunk, rank)
    g_line = line_reduce(g_src, g_buf, g_sem)

    ring[4].wait_recv()
    ring["4b"].wait_recv()
    across[4] = b_sibling(4)
    across[6].wait_recv()
    across[3].wait_recv()
    columns([(6, 0), (6, 1), (3, 0), (3, 1)])
    across[5].wait_recv()
    across[4].wait_recv()
    columns([(5, 0), (5, 1), (4, 0), (4, 1)])

    part[...] = part[...] * amp
    part[:n_rows, :] = part[:n_rows, :] + noise * probes_ref[...]
    hi, lo = split(part[...])
    both = dot_nn(ct_hi[...], jnp.concatenate([hi, lo], axis=1))
    q = both[:, :n_probe] + both[:, n_probe:] + dot_nn(ct_lo[...], hi)
    q_all[...] = q.reshape(NC, PLANE, chunk, n_probe)
    q1 = plane_scatter(q_all, q1_buf, q1_sem)

    landed(g_line)
    gram[my_rows(core), :] = summed(g_src[core], g_buf, LINE)
    g_plane = plane_gather(gram, g_sem)
    s = dot_nt(r_cat[:n_rows, :], piv_cat[...])
    cross_own[...] = amp * matern(s + twice(r_norm[:n_rows, :]) + piv_norm_row)
    hi, lo = split(pv * -2.0)
    s = dot_nt(jnp.concatenate([hi, hi, lo], axis=1), piv_cat[...])
    full[...] = (noise * amp) * matern(s + twice(piv_norm) + piv_norm_row)

    landed(q1)
    q_src[...] = summed(q_all[:, here], q1_buf, PLANE)
    q_line = line_reduce(q_src, q_buf, q_sem)
    landed(g_plane)
    r_copies = []
    for dx, dy in plane_offsets:
        k = dy * NX + dx
        source = part.at[pl.ds(k * n_rows, n_rows)]
        r_copies.append(send(source, prod_buf.at[k], r_sem, k, plane(-dx, -dy)[0]))
    full[...] = full[...] + gram[...]

    half = rank // 2
    tiles = half // 8
    work[...] = full[:half, :half].reshape(tiles, 8, half)
    invert(work)
    landed(q_line)
    q_out[my_rows(core), :] = summed(q_src[core], q_buf, LINE)
    q_plane = plane_gather(q_out, q_sem)
    upper_inverse = work[...].reshape(half, half)
    lower = full[half:, :half]
    carried = dot_exact(upper_inverse, full[:half, half:])
    work[...] = (full[half:, half:] - dot_exact(lower, carried)).reshape(tiles, 8, half)
    invert(work)
    landed(q_plane)
    lower_inverse = work[...].reshape(half, half)

    def solved(right_side):
        top = dot_exact(upper_inverse, right_side[:half])
        below = dot_exact(lower_inverse, right_side[half:] - dot_exact(lower, top))
        return jnp.concatenate([top - dot_exact(carried, below), below], axis=0)

    projected = q_out[...]
    coefficients = solved(projected)
    coefficients = coefficients + solved(projected - dot_exact(full[...], coefficients))
    landed(r_copies)
    product = summed(part[:n_rows, :], prod_buf, PLANE)
    product_ref[...] = product
    removed = dot_exact(cross_own[...], coefficients)
    out_ref[...] = (product - removed) / noise

    for c in everything:
        c.wait_send()


def per_device(features, probes, outputscale, noise, pivots):
    n_rows, n_feat = features.shape
    n_probe = probes.shape[1]
    rank = pivots.shape[0]
    chunk = rank // NC // PLANE
    wide = PLANE * n_rows
    block = 4 * n_rows
    vmem = pltpu.VMEM
    dma = pltpu.SemaphoreType.DMA
    spread = jnp.broadcast_to(pivots[:, None], (rank, 128))
    return pl.pallas_call(
        exchange_kernel,
        out_shape=(jax.ShapeDtypeStruct((n_rows, n_probe), f32),) * 2,
        in_specs=[pl.BlockSpec(memory_space=vmem)] * 3
        + [pl.BlockSpec(memory_space=pltpu.SMEM)] * 2,
        out_specs=[pl.BlockSpec(memory_space=vmem)] * 2,
        scratch_shapes=[
            vmem((2, NY, NX, n_rows, n_feat // 2), f32),
            vmem((LINE, n_rows, n_feat + n_probe), f32),
            vmem((NC, PLANE, chunk, n_feat), f32),
            vmem((PLANE, NC, chunk, n_feat), f32),
            vmem((NC, chunk, n_feat), f32),
            vmem((LINE, chunk, n_feat), f32),
            vmem((rank, n_feat), f32),
            vmem((wide, 3 * n_feat), bf16),
            vmem((wide, 128), f32),
            vmem((1, wide), f32),
            vmem((block, 3 * n_feat), bf16),
            vmem((1, block), f32),
            vmem((block, 2 * n_probe), bf16),
            vmem((wide, n_probe), f32),
            vmem((rank, 3 * n_feat), bf16),
            vmem((rank, wide), f32),
            vmem((rank, wide), bf16),
            vmem((rank, wide), bf16),
            vmem((n_rows, rank), f32),
            vmem((NC, chunk, rank), f32),
            vmem((LINE, chunk, rank), f32),
            vmem((rank, rank), f32),
            vmem((NC, PLANE, chunk, n_probe), f32),
            vmem((PLANE, NC, chunk, n_probe), f32),
            vmem((NC, chunk, n_probe), f32),
            vmem((LINE, chunk, n_probe), f32),
            vmem((rank, n_probe), f32),
            vmem((PLANE, n_rows, n_probe), f32),
            vmem((rank // 16, 8, rank // 2), f32),
            vmem((rank, rank), f32),
            dma((2, 2 * PLANE)),
            dma((2, LINE + 1)),
            dma((2, LINE + 2 * PLANE)),
            dma((2, LINE + 2 * PLANE)),
            dma((2, LINE + 2 * PLANE)),
            dma((2, PLANE)),
            dma((2, PLANE)),
            dma((2, PLANE)),
        ],
        compiler_params=pltpu.CompilerParams(
            collective_id=0, has_side_effects=True, vmem_limit_bytes=40 * 1024 * 1024
        ),
        name="exchange",
    )(features, probes, spread, outputscale, noise)


def solution(mesh):
    in_specs = (P(("blk", "row"), None), P(("blk", "row"), None), P(), P(), P())
    out_specs = (P(("blk", "row"), None), P(("blk", "row"), None))
    return jax.shard_map(
        per_device, mesh=mesh, in_specs=in_specs, out_specs=out_specs, check_vma=False
    )
```

```python
import jax
import jax.numpy as jnp
from jax import lax
from jax.experimental import pallas as pl
from jax.experimental.pallas import tpu as pltpu
from jax.sharding import PartitionSpec as P

MESH = pl.DeviceIdType.MESH
highest = lax.Precision.HIGHEST
root_five = 2.23606797749979
f32 = jnp.float32
bf16 = jnp.bfloat16

NX, NY, NZ, NC = 4, 4, 8, 2
ZLO = 4
PLANE = NX * NY
LINE = NZ * NC


def split(x):
    hi = x.astype(bf16)
    return hi, (x - hi.astype(f32)).astype(bf16)


def dot_nt(a, b):
    return lax.dot_general(a, b, (((1,), (1,)), ((), ())), preferred_element_type=f32)


def dot_nn(a, b):
    return jnp.dot(a, b, preferred_element_type=f32)


def matern(scaled_square):
    s = jnp.maximum(scaled_square, 1e-30)
    t = s * lax.rsqrt(s)
    return (1.0 + t + s * (1.0 / 3.0)) * jnp.exp(-t)


def column_norms(x):
    return jnp.broadcast_to(jnp.sum(x * x, axis=1, keepdims=True), (x.shape[0], 128))


def as_row(norms):
    return jnp.transpose(norms)[0:1]


def twice(x):
    return jnp.concatenate([x, x], axis=1)


def dot_exact(a, b):
    return jnp.dot(a, b, precision=highest, preferred_element_type=f32)


def invert(work):
    tiles, _, half = work.shape
    sub = lax.broadcasted_iota(jnp.int32, (8, half), 0)
    lane = lax.broadcasted_iota(jnp.int32, (8, half), 1)

    def spread_lane(v, c):
        return jnp.take_along_axis(v, jnp.full((8, half), c, jnp.int32), axis=1)

    def spread_row(v, r):
        return jnp.broadcast_to(v[r:r + 1, :], v.shape)

    def reciprocal(d):
        r = pl.reciprocal(d, approx=True)
        r = r * (2.0 - d * r)
        return r * (2.0 - d * r)

    def in_block(block):
        return (lane >= block * 8) & (lane < block * 8 + 8)

    def eliminated(top, block):
        d = [spread_lane(top, 8 * block + c) for c in range(8)]
        top = jnp.where(in_block(block), jnp.where(lane - block * 8 == sub, 1.0, 0.0), top)
        for s in range(0, 8, 2):
            a, b, c = spread_row(d[s], s), spread_row(d[s + 1], s), spread_row(d[s + 1], s + 1)
            inverse = reciprocal(a * c - b * b)
            first, second = d[s], d[s + 1]

            def swept(v):
                r0, r1 = spread_row(v, s), spread_row(v, s + 1)
                n0 = c * r0 - b * r1
                n1 = a * r1 - b * r0
                taken = jnp.where(sub == s, n0, jnp.where(sub == s + 1, n1, -(first * n0 + second * n1)))
                kept = jnp.where((sub == s) | (sub == s + 1), 0.0, v)
                return kept + taken * inverse

            for c2 in range(s + 2, 8):
                d[c2] = swept(d[c2])
            top = swept(top)
        return top

    def updated(v, block, rows):
        total = jnp.where(in_block(block), 0.0, v)
        for c in range(8):
            total = total - spread_lane(v, 8 * block + c) * rows[c]
        return total

    panel = tiles // 4
    for p in range(0, tiles, panel):
        block_rows = [work[p + i] for i in range(panel)]
        for i in range(panel):
            done = eliminated(block_rows[i], p + i)
            rows = [spread_row(done, c) for c in range(8)]
            for other in range(panel):
                if other != i:
                    block_rows[other] = updated(block_rows[other], p + i, rows)
            block_rows[i] = done
        reduced = jnp.concatenate(block_rows, axis=0)
        whole = work[...].reshape(half, half)
        first, last = 8 * p, 8 * (p + panel)
        column = lax.broadcasted_iota(jnp.int32, (half, half), 1)
        rest = jnp.where((column >= first) & (column < last), 0.0, whole)
        rest = rest - dot_exact(whole[:, first:last], reduced)
        work[...] = rest.reshape(tiles, 8, half)
        for i in range(panel):
            work[p + i] = block_rows[i]


def exchange_kernel(
    feats_ref, probes_ref, pivots_ref, amp_ref, noise_ref,
    product_ref, out_ref,
    a_buf, b_buf, pick, p1_buf, p_src, p_buf, piv,
    r_cat, r_norm, r_norm_row, c_cat, c_norm_row, v_cat, part,
    piv_cat, ct, ct_hi, ct_lo, cross_own, g_src, g_buf, gram, q_all, q1_buf, q_src, q_buf, q_out, prod_buf, work, full,
    a_sem, b_sem, stage_sem,
):
    n_rows, n_feat = feats_ref.shape
    n_probe = probes_ref.shape[1]
    rank = pivots_ref.shape[0]
    half_rank = rank // NC
    chunk = half_rank // PLANE
    half_feat = n_feat // 2
    blk, row = lax.axis_index("blk"), lax.axis_index("row")
    core = lax.rem(blk, NC)
    y = lax.rem(lax.div(blk, NC), NY)
    x = lax.rem(row, NX)
    z = lax.div(row, NX) * ZLO + lax.div(blk, NC * NY)
    here = y * NX + x

    def plane(dx, dy):
        xx, yy = lax.rem(x + (dx + NX), NX), lax.rem(y + (dy + NY), NY)
        return ((lax.div(blk, NC * NY) * NY + yy) * NC + core, lax.div(row, NX) * NX + xx), yy * NX + xx

    def line(dz, dc):
        zz, cc = lax.rem(z + (dz + NZ), NZ), lax.rem(core + dc, NC)
        return ((lax.rem(zz, ZLO) * NY + y) * NC + cc, lax.div(zz, ZLO) * NX + x), cc

    plane_offsets = sorted(
        [(dx, dy) for dx in range(NX) for dy in range(NY) if dx or dy],
        key=lambda o: -(min(o[0], NX - o[0]) + min(o[1], NY - o[1])),
    )
    line_offsets = sorted(
        [(dz, dc) for dz in range(NZ) for dc in range(NC) if dz or dc],
        key=lambda o: -min(o[0], NZ - o[0]),
    )

    def send(src, dst, sem, k, device):
        copy = pltpu.make_async_remote_copy(
            src_ref=src, dst_ref=dst, send_sem=sem.at[0, k], recv_sem=sem.at[1, k],
            device_id=device, device_id_type=MESH,
        )
        copy.start()
        return copy

    barrier = pltpu.get_barrier_semaphore()
    for dx, dy in plane_offsets:
        pl.semaphore_signal(barrier, inc=1, device_id=plane(dx, dy)[0], device_id_type=MESH)
    for dz, dc in line_offsets:
        pl.semaphore_signal(barrier, inc=1, device_id=line(dz, dc)[0], device_id_type=MESH)

    amp, noise = amp_ref[0], noise_ref[0]
    own = feats_ref[...] * root_five
    a_buf[0, 0, 0] = own[:, :half_feat]
    a_buf[1, 0, 0] = own[:, half_feat:]
    b_buf[0, :, :n_feat] = own
    b_buf[0, :, n_feat:] = probes_ref[...]
    first = (blk * (NX * NZ // ZLO) + row) * n_rows
    point = lax.broadcasted_iota(jnp.int32, (rank, n_rows), 1) + first
    onehot = (point == pivots_ref[:, :n_rows]).astype(f32)
    pick[...] = dot_exact(onehot, own).reshape(NC, PLANE, chunk, n_feat)
    pl.semaphore_wait(barrier, PLANE + LINE - 2)

    upper_rows, lower_rows = pl.ds(0, n_rows // 2), pl.ds(n_rows // 2, n_rows // 2)

    moved = {}

    def a_slot(h, u, v):
        return a_buf.at[(h, v, u) if h == 0 else (h, u, v)]

    def a_send(h, u, v, du, dv):
        to = ((u + du) % 4, (v + dv) % 4)
        device = plane(du, dv)[0] if h == 0 else plane(dv, du)[0]
        moved[(h, *to)] = send(a_slot(h, u, v), a_slot(h, *to), a_sem, 16 * h + 4 * to[0] + to[1], device)

    def a_wait(*slots):
        for u, v in slots:
            for h in range(2):
                moved[(h, u, v)].wait_recv()

    def a_start():
        for d in (1, -1, 2):
            for h in range(2):
                a_send(h, 0, 0, d, 0)
                a_send(h, 0, 0, 0, d)

    def a_forward(*steps):
        for d in (1, -1, 2):
            for h in range(2):
                for u in steps:
                    a_send(h, u, 0, 0, d)

    right, left = line(1, 0)[0], line(-1, 0)[0]
    sibling = line(0, 1)[0]

    def b_slot(dz, dc):
        return b_buf.at[dz * NC + dc]

    def b_send(dz_from, dz_to, device):
        return send(b_slot(dz_from, 0), b_slot(dz_to, 0), b_sem, dz_to * NC, device)

    def b_sibling(dz):
        return send(b_slot(dz, 0), b_slot(dz, 1), b_sem, dz * NC + 1, sibling)

    def forward(step):
        ring[step].wait_recv()
        ring[8 - step].wait_recv()
        if step < 3:
            ring[step + 1] = b_send(step, step + 1, right)
            ring[7 - step] = b_send(8 - step, 7 - step, left)
        else:
            ring[4] = send(b_slot(3, 0).at[upper_rows], b_slot(4, 0).at[upper_rows], b_sem, 8, right)
            ring["4b"] = send(b_slot(5, 0).at[lower_rows], b_slot(4, 0).at[lower_rows], b_sem, LINE, left)
        across[step] = b_sibling(step)
        across[8 - step] = b_sibling(8 - step)

    def prepare(slots):
        for dx, dy in slots:
            k = dy * NX + dx
            rows = slice(k * n_rows, (k + 1) * n_rows)
            total = None
            for h in range(2):
                value = a_buf[h, dy, dx]
                hi, lo = split(value * -2.0)
                r_cat[rows, h * half_feat:(h + 1) * half_feat] = hi
                r_cat[rows, n_feat + h * half_feat:n_feat + (h + 1) * half_feat] = hi
                r_cat[rows, 2 * n_feat + h * half_feat:2 * n_feat + (h + 1) * half_feat] = lo
                square = value * value
                total = square if total is None else total + square
            r_norm[rows, :] = jnp.broadcast_to(jnp.sum(total, axis=1, keepdims=True), (n_rows, 128))

    def my_rows(c):
        return pl.ds(pl.multiple_of(c * half_rank + here * chunk, chunk), chunk)

    def stage(copies, number, whole):
        for src, dst, device in copies:
            pltpu.make_async_remote_copy(
                src_ref=src, dst_ref=dst, send_sem=stage_sem.at[0, number], recv_sem=stage_sem.at[1, number],
                device_id=device, device_id_type=MESH,
            ).start()
        return pltpu.make_async_remote_copy(
            src_ref=whole, dst_ref=whole, send_sem=stage_sem.at[0, number], recv_sem=stage_sem.at[1, number],
            device_id=sibling, device_id_type=MESH,
        )

    def line_reduce(src, dst, number):
        copies = []
        for dz, dc in line_offsets:
            device, cc = line(dz, dc)
            copies.append((src.at[cc], dst.at[dz * NC + dc], device))
        return stage(copies, number, dst.at[pl.ds(1, LINE - 1)])

    def plane_gather(ref, number):
        copies = []
        mine = ref.at[my_rows(core)]
        for dx, dy in plane_offsets:
            (other_blk, other_row), _ = plane(dx, dy)
            copies.append((mine, mine, (other_blk, other_row)))
            copies.append((mine, mine, (other_blk + 1 - 2 * core, other_row)))
        copies.append((mine, mine, sibling))
        return stage(copies, number, ref.at[pl.ds(0, len(copies) * chunk)])

    def plane_scatter(src, dst, number):
        copies = []
        for dx, dy in plane_offsets:
            device, there = plane(dx, dy)
            copies.append((src.at[:, there], dst.at[dy * NX + dx], device))
        return stage(copies, number, dst.at[pl.ds(1, PLANE - 1)])

    def summed(total, buf, count):
        for k in range(1, count):
            total = total + buf[k]
        return total

    p_scatter = plane_scatter(pick, p1_buf, 0)
    ring = {1: b_send(0, 1, right), 7: b_send(0, 7, left)}
    across = {0: b_sibling(0)}
    a_start()
    prepare([(0, 0)])
    a_wait((1, 0), (3, 0))
    a_forward(1, 3)
    forward(1)
    a_wait((2, 0))
    a_forward(2)
    p_scatter.wait_recv()
    p_src[...] = summed(pick[:, here], p1_buf, PLANE)
    p_line = line_reduce(p_src, p_buf, 1)
    a_wait((0, 1), (0, 3), (0, 2))
    prepare([(1, 0), (3, 0), (2, 0), (0, 1), (0, 3), (0, 2)])
    forward(2)
    p_line.wait_recv()
    piv[my_rows(core), :] = summed(p_src[core], p_buf, LINE)
    p_plane = plane_gather(piv, 2)
    a_wait((1, 1), (1, 3), (3, 1), (3, 3), (1, 2), (3, 2), (2, 1), (2, 3), (2, 2))
    prepare([(1, 1), (1, 3), (3, 1), (3, 3), (2, 1), (2, 3), (1, 2), (3, 2), (2, 2)])
    forward(3)

    for k in range(0, r_norm.shape[0], 128):
        r_norm_row[:, k:k + 128] = as_row(r_norm[k:k + 128, :])
    part[...] = jnp.zeros_like(part)
    tile = 256

    def columns(slots):
        for i, (dz, dc) in enumerate(slots):
            rows = slice(i * n_rows, (i + 1) * n_rows)
            value = b_buf[dz * NC + dc, :, :n_feat]
            hi, lo = split(value)
            c_cat[rows, :n_feat] = hi
            c_cat[rows, n_feat:2 * n_feat] = lo
            c_cat[rows, 2 * n_feat:] = hi
            hi, lo = split(b_buf[dz * NC + dc, :, n_feat:])
            v_cat[rows, :n_probe] = hi
            v_cat[rows, n_probe:] = lo
        for i in range(0, len(slots), 2):
            pair = [column_norms(b_buf[dz * NC + dc, :, :n_feat]) for dz, dc in slots[i:i + 2]]
            c_norm_row[:, i * n_rows:(i + 2) * n_rows] = as_row(jnp.concatenate(pair, axis=0))

        def body(i, carry):
            rows = pl.ds(pl.multiple_of(i * tile, tile), tile)
            s = dot_nt(r_cat[rows, :], c_cat[...])
            k = matern(s + twice(r_norm[rows, :]) + c_norm_row[...])
            hi, lo = split(k)
            both = dot_nn(hi, v_cat[...])
            last = dot_nn(lo, v_cat[:, :n_probe])
            part[rows, :] = part[rows, :] + (both[:, :n_probe] + both[:, n_probe:] + last)
            return carry

        lax.fori_loop(0, part.shape[0] // tile, body, 0, unroll=2)

    across[0].wait_recv()
    across[1].wait_recv()
    columns([(0, 0), (0, 1), (1, 0), (1, 1)])

    across[2].wait_recv()
    across[7].wait_recv()
    columns([(7, 0), (7, 1), (2, 0), (2, 1)])
    for c in list(moved.values()) + [ring[k] for k in (1, 2, 3, 5, 6, 7)]:
        c.wait_send()
    p_scatter.wait_send()
    p_line.wait_send()
    p_plane.wait_recv()
    pv = piv[...]
    hi, lo = split(pv)
    piv_cat[:, :n_feat] = hi
    piv_cat[:, n_feat:2 * n_feat] = lo
    piv_cat[:, 2 * n_feat:] = hi
    piv_norm = column_norms(pv)
    piv_norm_row = jnp.concatenate([as_row(piv_norm[k:k + 128]) for k in range(0, rank, 128)], axis=1)
    for i in range(r_cat.shape[0] // tile):
        rows = slice(i * tile, (i + 1) * tile)
        s = dot_nt(piv_cat[...], r_cat[rows, :])
        value = amp * matern(s + twice(piv_norm) + r_norm_row[:, rows])
        ct[:, rows] = value
        hi, lo = split(value)
        ct_hi[:, rows] = hi
        ct_lo[:, rows] = lo
    hi, lo = split(jnp.concatenate([ct[my_rows(c), :] for c in range(NC)], axis=0))
    both = dot_nt(jnp.concatenate([hi, lo], axis=0), ct_hi[...])
    g = both[:NC * chunk] + both[NC * chunk:] + dot_nt(hi, ct_lo[...])
    g_src[...] = g.reshape(NC, chunk, rank)
    g_line = line_reduce(g_src, g_buf, 3)

    ring[4].wait_recv()
    ring["4b"].wait_recv()
    across[4] = b_sibling(4)
    across[6].wait_recv()
    across[3].wait_recv()
    columns([(6, 0), (6, 1), (3, 0), (3, 1)])
    across[5].wait_recv()
    across[4].wait_recv()
    columns([(5, 0), (5, 1), (4, 0), (4, 1)])

    part[...] = part[...] * amp
    part[:n_rows, :] = part[:n_rows, :] + noise * probes_ref[...]
    hi, lo = split(part[...])
    both = dot_nn(ct_hi[...], jnp.concatenate([hi, lo], axis=1))
    q = both[:, :n_probe] + both[:, n_probe:] + dot_nn(ct_lo[...], hi)
    q_all[...] = q.reshape(NC, PLANE, chunk, n_probe)
    q1 = plane_scatter(q_all, q1_buf, 5)

    for step in (4, "4b"):
        ring[step].wait_send()
    for copy in across.values():
        copy.wait_send()
    p_plane.wait_send()
    g_line.wait_recv()
    gram[my_rows(core), :] = summed(g_src[core], g_buf, LINE)
    g_plane = plane_gather(gram, 4)
    s = dot_nt(r_cat[:n_rows, :], piv_cat[...])
    cross_own[...] = amp * matern(s + twice(r_norm[:n_rows, :]) + piv_norm_row)
    hi, lo = split(pv * -2.0)
    s = dot_nt(jnp.concatenate([hi, hi, lo], axis=1), piv_cat[...])
    full[...] = (noise * amp) * matern(s + twice(piv_norm) + piv_norm_row)

    g_line.wait_send()
    q1.wait_recv()
    q_src[...] = summed(q_all[:, here], q1_buf, PLANE)
    q_line = line_reduce(q_src, q_buf, 6)
    g_plane.wait_recv()
    r_copies = []
    for dx, dy in plane_offsets:
        k = dy * NX + dx
        source = part.at[pl.ds(k * n_rows, n_rows)]
        r_copies.append((source, prod_buf.at[k], plane(-dx, -dy)[0]))
    r_stage = stage(r_copies, 8, prod_buf.at[pl.ds(1, PLANE - 1)])
    full[...] = full[...] + gram[...]

    half = rank // 2
    tiles = half // 8
    work[...] = full[:half, :half].reshape(tiles, 8, half)
    invert(work)
    q_line.wait_recv()
    q_out[my_rows(core), :] = summed(q_src[core], q_buf, LINE)
    q_plane = plane_gather(q_out, 7)
    upper_inverse = work[...].reshape(half, half)
    lower = full[half:, :half]
    carried = dot_exact(upper_inverse, full[:half, half:])
    work[...] = (full[half:, half:] - dot_exact(lower, carried)).reshape(tiles, 8, half)
    invert(work)
    for later in (g_plane, q1, q_line, r_stage):
        later.wait_send()
    q_plane.wait_recv()
    lower_inverse = work[...].reshape(half, half)

    def solved(right_side):
        top = dot_exact(upper_inverse, right_side[:half])
        below = dot_exact(lower_inverse, right_side[half:] - dot_exact(lower, top))
        return jnp.concatenate([top - dot_exact(carried, below), below], axis=0)

    projected = q_out[...]
    coefficients = solved(projected)
    coefficients = coefficients + solved(projected - dot_exact(full[...], coefficients))
    r_stage.wait_recv()
    product = summed(part[:n_rows, :], prod_buf, PLANE)
    product_ref[...] = product
    removed = dot_exact(cross_own[...], coefficients)
    out_ref[...] = (product - removed) / noise

    q_plane.wait_send()


def per_device(features, probes, outputscale, noise, pivots):
    n_rows, n_feat = features.shape
    n_probe = probes.shape[1]
    rank = pivots.shape[0]
    chunk = rank // NC // PLANE
    wide = PLANE * n_rows
    block = 4 * n_rows
    vmem = pltpu.VMEM
    dma = pltpu.SemaphoreType.DMA
    spread = jnp.broadcast_to(pivots[:, None], (rank, 128))
    return pl.pallas_call(
        exchange_kernel,
        out_shape=(jax.ShapeDtypeStruct((n_rows, n_probe), f32),) * 2,
        in_specs=[pl.BlockSpec(memory_space=vmem)] * 3
        + [pl.BlockSpec(memory_space=pltpu.SMEM)] * 2,
        out_specs=[pl.BlockSpec(memory_space=vmem)] * 2,
        scratch_shapes=[
            vmem((2, NY, NX, n_rows, n_feat // 2), f32),
            vmem((LINE, n_rows, n_feat + n_probe), f32),
            vmem((NC, PLANE, chunk, n_feat), f32),
            vmem((PLANE, NC, chunk, n_feat), f32),
            vmem((NC, chunk, n_feat), f32),
            vmem((LINE, chunk, n_feat), f32),
            vmem((rank, n_feat), f32),
            vmem((wide, 3 * n_feat), bf16),
            vmem((wide, 128), f32),
            vmem((1, wide), f32),
            vmem((block, 3 * n_feat), bf16),
            vmem((1, block), f32),
            vmem((block, 2 * n_probe), bf16),
            vmem((wide, n_probe), f32),
            vmem((rank, 3 * n_feat), bf16),
            vmem((rank, wide), f32),
            vmem((rank, wide), bf16),
            vmem((rank, wide), bf16),
            vmem((n_rows, rank), f32),
            vmem((NC, chunk, rank), f32),
            vmem((LINE, chunk, rank), f32),
            vmem((rank, rank), f32),
            vmem((NC, PLANE, chunk, n_probe), f32),
            vmem((PLANE, NC, chunk, n_probe), f32),
            vmem((NC, chunk, n_probe), f32),
            vmem((LINE, chunk, n_probe), f32),
            vmem((rank, n_probe), f32),
            vmem((PLANE, n_rows, n_probe), f32),
            vmem((rank // 16, 8, rank // 2), f32),
            vmem((rank, rank), f32),
            dma((2, 2 * PLANE)),
            dma((2, LINE + 1)),
            dma((2, 9)),
        ],
        compiler_params=pltpu.CompilerParams(
            collective_id=0, has_side_effects=True, vmem_limit_bytes=40 * 1024 * 1024
        ),
        name="exchange",
    )(features, probes, spread, outputscale, noise)


def solution(mesh):
    in_specs = (P(("blk", "row"), None), P(("blk", "row"), None), P(), P(), P())
    out_specs = (P(("blk", "row"), None), P(("blk", "row"), None))
    return jax.shard_map(
        per_device, mesh=mesh, in_specs=in_specs, out_specs=out_specs, check_vma=False
    )
```

```python
import jax
import jax.numpy as jnp
from jax import lax
from jax.experimental import pallas as pl
from jax.experimental.pallas import tpu as pltpu
from jax.sharding import PartitionSpec as P

MESH = pl.DeviceIdType.MESH
highest = lax.Precision.HIGHEST
root_five = 2.23606797749979
f32 = jnp.float32
bf16 = jnp.bfloat16

NX, NY, NZ, NC = 4, 4, 8, 2
ZLO = 4
PLANE = NX * NY
LINE = NZ * NC


def split(x):
    hi = x.astype(bf16)
    return hi, (x - hi.astype(f32)).astype(bf16)


def dot_nt(a, b):
    return lax.dot_general(a, b, (((1,), (1,)), ((), ())), preferred_element_type=f32)


def dot_nn(a, b):
    return jnp.dot(a, b, preferred_element_type=f32)


def matern(scaled_square):
    s = jnp.maximum(scaled_square, 1e-30)
    t = s * lax.rsqrt(s)
    return (1.0 + t + s * (1.0 / 3.0)) * jnp.exp(-t)


def column_norms(x):
    return jnp.broadcast_to(jnp.sum(x * x, axis=1, keepdims=True), (x.shape[0], 128))


def as_row(norms):
    return jnp.transpose(norms)[0:1]


def twice(x):
    return jnp.concatenate([x, x], axis=1)


def dot_exact(a, b):
    return jnp.dot(a, b, precision=highest, preferred_element_type=f32)


def invert(work):
    tiles, _, half = work.shape
    sub = lax.broadcasted_iota(jnp.int32, (8, half), 0)
    lane = lax.broadcasted_iota(jnp.int32, (8, half), 1)

    def spread_lane(v, c):
        return jnp.take_along_axis(v, jnp.full((8, half), c, jnp.int32), axis=1)

    def spread_row(v, r):
        return jnp.broadcast_to(v[r:r + 1, :], v.shape)

    def reciprocal(d):
        r = pl.reciprocal(d, approx=True)
        r = r * (2.0 - d * r)
        return r * (2.0 - d * r)

    def in_block(block):
        return (lane >= block * 8) & (lane < block * 8 + 8)

    def eliminated(top, block):
        d = [spread_lane(top, 8 * block + c) for c in range(8)]
        top = jnp.where(in_block(block), jnp.where(lane - block * 8 == sub, 1.0, 0.0), top)
        for s in range(0, 8, 2):
            a, b, c = spread_row(d[s], s), spread_row(d[s + 1], s), spread_row(d[s + 1], s + 1)
            inverse = reciprocal(a * c - b * b)
            first, second = d[s], d[s + 1]

            def swept(v):
                r0, r1 = spread_row(v, s), spread_row(v, s + 1)
                n0 = c * r0 - b * r1
                n1 = a * r1 - b * r0
                taken = jnp.where(sub == s, n0, jnp.where(sub == s + 1, n1, -(first * n0 + second * n1)))
                kept = jnp.where((sub == s) | (sub == s + 1), 0.0, v)
                return kept + taken * inverse

            for c2 in range(s + 2, 8):
                d[c2] = swept(d[c2])
            top = swept(top)
        return top

    def updated(v, block, rows):
        total = jnp.where(in_block(block), 0.0, v)
        for c in range(8):
            total = total - spread_lane(v, 8 * block + c) * rows[c]
        return total

    panel = tiles // 4
    for p in range(0, tiles, panel):
        block_rows = [work[p + i] for i in range(panel)]
        for i in range(panel):
            done = eliminated(block_rows[i], p + i)
            rows = [spread_row(done, c) for c in range(8)]
            for other in range(panel):
                if other != i:
                    block_rows[other] = updated(block_rows[other], p + i, rows)
            block_rows[i] = done
        reduced = jnp.concatenate(block_rows, axis=0)
        whole = work[...].reshape(half, half)
        first, last = 8 * p, 8 * (p + panel)
        column = lax.broadcasted_iota(jnp.int32, (half, half), 1)
        rest = jnp.where((column >= first) & (column < last), 0.0, whole)
        rest = rest - dot_exact(whole[:, first:last], reduced)
        work[...] = rest.reshape(tiles, 8, half)
        for i in range(panel):
            work[p + i] = block_rows[i]


def exchange_kernel(
    feats_ref, probes_ref, pivots_ref, amp_ref, noise_ref,
    product_ref, own_ref, out_ref,
    a_buf, b_buf, pick, p1_buf, p_src, p_buf, piv,
    r_cat, r_norm, r_norm_row, c_cat, c_norm_row, v_cat, part,
    piv_cat, ct, ct_hi, ct_lo, cross_own, g_src, g_buf, gram, q_all, q1_buf, q_src, q_buf, q_out, prod_buf, work, full,
    a_sem, b_sem, stage_sem,
):
    n_rows, n_feat = feats_ref.shape
    n_probe = probes_ref.shape[1]
    rank = pivots_ref.shape[0]
    half_rank = rank // NC
    chunk = half_rank // PLANE
    half_feat = n_feat // 2
    blk, row = lax.axis_index("blk"), lax.axis_index("row")
    core = lax.rem(blk, NC)
    y = lax.rem(lax.div(blk, NC), NY)
    x = lax.rem(row, NX)
    z = lax.div(row, NX) * ZLO + lax.div(blk, NC * NY)
    here = y * NX + x

    def plane(dx, dy):
        xx, yy = lax.rem(x + (dx + NX), NX), lax.rem(y + (dy + NY), NY)
        return ((lax.div(blk, NC * NY) * NY + yy) * NC + core, lax.div(row, NX) * NX + xx), yy * NX + xx

    def line(dz, dc):
        zz, cc = lax.rem(z + (dz + NZ), NZ), lax.rem(core + dc, NC)
        return ((lax.rem(zz, ZLO) * NY + y) * NC + cc, lax.div(zz, ZLO) * NX + x), cc

    plane_offsets = sorted(
        [(dx, dy) for dx in range(NX) for dy in range(NY) if dx or dy],
        key=lambda o: -(min(o[0], NX - o[0]) + min(o[1], NY - o[1])),
    )
    line_offsets = sorted(
        [(dz, dc) for dz in range(NZ) for dc in range(NC) if dz or dc],
        key=lambda o: -min(o[0], NZ - o[0]),
    )

    def send(src, dst, sem, k, device):
        copy = pltpu.make_async_remote_copy(
            src_ref=src, dst_ref=dst, send_sem=sem.at[0, k], recv_sem=sem.at[1, k],
            device_id=device, device_id_type=MESH,
        )
        copy.start()
        return copy

    barrier = pltpu.get_barrier_semaphore()
    for dx, dy in plane_offsets:
        pl.semaphore_signal(barrier, inc=1, device_id=plane(dx, dy)[0], device_id_type=MESH)
    for dz, dc in line_offsets:
        pl.semaphore_signal(barrier, inc=1, device_id=line(dz, dc)[0], device_id_type=MESH)

    amp, noise = amp_ref[0], noise_ref[0]
    own = feats_ref[...] * root_five
    a_buf[0, 0, 0] = own[:, :half_feat]
    a_buf[1, 0, 0] = own[:, half_feat:]
    b_buf[0, :, :n_feat] = own
    b_buf[0, :, n_feat:] = probes_ref[...]
    first = (blk * (NX * NZ // ZLO) + row) * n_rows
    point = lax.broadcasted_iota(jnp.int32, (rank, n_rows), 1) + first
    onehot = (point == pivots_ref[:, :n_rows]).astype(f32)
    pick[...] = dot_exact(onehot, own).reshape(NC, PLANE, chunk, n_feat)
    pl.semaphore_wait(barrier, PLANE + LINE - 2)

    upper_rows, lower_rows = pl.ds(0, n_rows // 2), pl.ds(n_rows // 2, n_rows // 2)

    moved = {}

    def a_slot(h, u, v):
        return a_buf.at[(h, v, u) if h == 0 else (h, u, v)]

    def a_send(h, u, v, du, dv):
        to = ((u + du) % 4, (v + dv) % 4)
        device = plane(du, dv)[0] if h == 0 else plane(dv, du)[0]
        moved[(h, *to)] = send(a_slot(h, u, v), a_slot(h, *to), a_sem, 16 * h + 4 * to[0] + to[1], device)

    def a_wait(*slots):
        for u, v in slots:
            for h in range(2):
                moved[(h, u, v)].wait_recv()

    def a_start():
        for d in (1, -1, 2):
            for h in range(2):
                a_send(h, 0, 0, d, 0)
                a_send(h, 0, 0, 0, d)

    def a_forward(*steps):
        for d in (1, -1, 2):
            for h in range(2):
                for u in steps:
                    a_send(h, u, 0, 0, d)

    right, left = line(1, 0)[0], line(-1, 0)[0]
    sibling = line(0, 1)[0]

    def b_slot(dz, dc):
        return b_buf.at[dz * NC + dc]

    def b_send(dz_from, dz_to, device):
        return send(b_slot(dz_from, 0), b_slot(dz_to, 0), b_sem, dz_to * NC, device)

    def b_sibling(dz):
        return send(b_slot(dz, 0), b_slot(dz, 1), b_sem, dz * NC + 1, sibling)

    def forward(step):
        ring[step].wait_recv()
        ring[8 - step].wait_recv()
        if step < 3:
            ring[step + 1] = b_send(step, step + 1, right)
            ring[7 - step] = b_send(8 - step, 7 - step, left)
        else:
            ring[4] = send(b_slot(3, 0).at[upper_rows], b_slot(4, 0).at[upper_rows], b_sem, 8, right)
            ring["4b"] = send(b_slot(5, 0).at[lower_rows], b_slot(4, 0).at[lower_rows], b_sem, LINE, left)
        across[step] = b_sibling(step)
        across[8 - step] = b_sibling(8 - step)

    def prepare(slots):
        for dx, dy in slots:
            k = dy * NX + dx
            rows = slice(k * n_rows, (k + 1) * n_rows)
            total = None
            for h in range(2):
                value = a_buf[h, dy, dx]
                hi, lo = split(value * -2.0)
                r_cat[rows, h * half_feat:(h + 1) * half_feat] = hi
                r_cat[rows, n_feat + h * half_feat:n_feat + (h + 1) * half_feat] = hi
                r_cat[rows, 2 * n_feat + h * half_feat:2 * n_feat + (h + 1) * half_feat] = lo
                square = value * value
                total = square if total is None else total + square
            r_norm[rows, :] = jnp.broadcast_to(jnp.sum(total, axis=1, keepdims=True), (n_rows, 128))

    def my_rows(c):
        return pl.ds(pl.multiple_of(c * half_rank + here * chunk, chunk), chunk)

    def stage(copies, number, whole):
        for src, dst, device in copies:
            pltpu.make_async_remote_copy(
                src_ref=src, dst_ref=dst, send_sem=stage_sem.at[0, number], recv_sem=stage_sem.at[1, number],
                device_id=device, device_id_type=MESH,
            ).start()
        return pltpu.make_async_remote_copy(
            src_ref=whole, dst_ref=whole, send_sem=stage_sem.at[0, number], recv_sem=stage_sem.at[1, number],
            device_id=sibling, device_id_type=MESH,
        )

    def line_reduce(src, dst, number):
        copies = []
        for dz, dc in line_offsets:
            device, cc = line(dz, dc)
            copies.append((src.at[cc], dst.at[dz * NC + dc], device))
        return stage(copies, number, dst.at[pl.ds(1, LINE - 1)])

    def plane_gather(ref, number):
        copies = []
        mine = ref.at[my_rows(core)]
        for dx, dy in plane_offsets:
            (other_blk, other_row), _ = plane(dx, dy)
            copies.append((mine, mine, (other_blk, other_row)))
            copies.append((mine, mine, (other_blk + 1 - 2 * core, other_row)))
        copies.append((mine, mine, sibling))
        return stage(copies, number, ref.at[pl.ds(0, len(copies) * chunk)])

    def plane_scatter(src, dst, number):
        copies = []
        for dx, dy in plane_offsets:
            device, there = plane(dx, dy)
            copies.append((src.at[:, there], dst.at[dy * NX + dx], device))
        return stage(copies, number, dst.at[pl.ds(1, PLANE - 1)])

    def summed(total, buf, count):
        for k in range(1, count):
            total = total + buf[k]
        return total

    p_scatter = plane_scatter(pick, p1_buf, 0)
    ring = {1: b_send(0, 1, right), 7: b_send(0, 7, left)}
    across = {0: b_sibling(0)}
    a_start()
    prepare([(0, 0)])
    a_wait((1, 0), (3, 0))
    a_forward(1, 3)
    forward(1)
    a_wait((2, 0))
    a_forward(2)
    p_scatter.wait_recv()
    p_src[...] = summed(pick[:, here], p1_buf, PLANE)
    p_line = line_reduce(p_src, p_buf, 1)
    a_wait((0, 1), (0, 3), (0, 2))
    prepare([(1, 0), (3, 0), (2, 0), (0, 1), (0, 3), (0, 2)])
    forward(2)
    p_line.wait_recv()
    piv[my_rows(core), :] = summed(p_src[core], p_buf, LINE)
    p_plane = plane_gather(piv, 2)
    a_wait((1, 1), (1, 3), (3, 1), (3, 3), (1, 2), (3, 2), (2, 1), (2, 3), (2, 2))
    prepare([(1, 1), (1, 3), (3, 1), (3, 3), (2, 1), (2, 3), (1, 2), (3, 2), (2, 2)])
    forward(3)

    for k in range(0, r_norm.shape[0], 128):
        r_norm_row[:, k:k + 128] = as_row(r_norm[k:k + 128, :])
    part[...] = jnp.zeros_like(part)
    tile = 256

    def columns(slots):
        for i, (dz, dc) in enumerate(slots):
            rows = slice(i * n_rows, (i + 1) * n_rows)
            value = b_buf[dz * NC + dc, :, :n_feat]
            hi, lo = split(value)
            c_cat[rows, :n_feat] = hi
            c_cat[rows, n_feat:2 * n_feat] = lo
            c_cat[rows, 2 * n_feat:] = hi
            hi, lo = split(b_buf[dz * NC + dc, :, n_feat:])
            v_cat[rows, :n_probe] = hi
            v_cat[rows, n_probe:] = lo
        for i in range(0, len(slots), 2):
            pair = [column_norms(b_buf[dz * NC + dc, :, :n_feat]) for dz, dc in slots[i:i + 2]]
            c_norm_row[:, i * n_rows:(i + 2) * n_rows] = as_row(jnp.concatenate(pair, axis=0))

        def body(i, carry):
            rows = pl.ds(pl.multiple_of(i * tile, tile), tile)
            s = dot_nt(r_cat[rows, :], c_cat[...])
            k = matern(s + twice(r_norm[rows, :]) + c_norm_row[...])
            hi, lo = split(k)
            both = dot_nn(hi, v_cat[...])
            last = dot_nn(lo, v_cat[:, :n_probe])
            part[rows, :] = part[rows, :] + (both[:, :n_probe] + both[:, n_probe:] + last)
            return carry

        lax.fori_loop(0, part.shape[0] // tile, body, 0, unroll=4)

    across[0].wait_recv()
    across[1].wait_recv()
    columns([(0, 0), (0, 1), (1, 0), (1, 1)])

    across[2].wait_recv()
    across[7].wait_recv()
    columns([(7, 0), (7, 1), (2, 0), (2, 1)])
    for c in list(moved.values()) + [ring[k] for k in (1, 2, 3, 5, 6, 7)]:
        c.wait_send()
    p_scatter.wait_send()
    p_line.wait_send()
    p_plane.wait_recv()
    pv = piv[...]
    hi, lo = split(pv)
    piv_cat[:, :n_feat] = hi
    piv_cat[:, n_feat:2 * n_feat] = lo
    piv_cat[:, 2 * n_feat:] = hi
    piv_norm = column_norms(pv)
    piv_norm_row = jnp.concatenate([as_row(piv_norm[k:k + 128]) for k in range(0, rank, 128)], axis=1)
    for i in range(r_cat.shape[0] // tile):
        rows = slice(i * tile, (i + 1) * tile)
        s = dot_nt(piv_cat[...], r_cat[rows, :])
        value = amp * matern(s + twice(piv_norm) + r_norm_row[:, rows])
        ct[:, rows] = value
        hi, lo = split(value)
        ct_hi[:, rows] = hi
        ct_lo[:, rows] = lo
    hi, lo = split(jnp.concatenate([ct[my_rows(c), :] for c in range(NC)], axis=0))
    both = dot_nt(jnp.concatenate([hi, lo], axis=0), ct_hi[...])
    g = both[:NC * chunk] + both[NC * chunk:] + dot_nt(hi, ct_lo[...])
    g_src[...] = g.reshape(NC, chunk, rank)
    g_line = line_reduce(g_src, g_buf, 3)

    ring[4].wait_recv()
    ring["4b"].wait_recv()
    across[4] = b_sibling(4)
    across[6].wait_recv()
    across[3].wait_recv()
    columns([(6, 0), (6, 1), (3, 0), (3, 1)])
    across[5].wait_recv()
    across[4].wait_recv()
    columns([(5, 0), (5, 1), (4, 0), (4, 1)])

    part[...] = part[...] * amp
    part[:n_rows, :] = part[:n_rows, :] + noise * probes_ref[...]
    hi, lo = split(part[...])
    both = dot_nn(ct_hi[...], jnp.concatenate([hi, lo], axis=1))
    q = both[:, :n_probe] + both[:, n_probe:] + dot_nn(ct_lo[...], hi)
    q_all[...] = q.reshape(NC, PLANE, chunk, n_probe)
    q1 = plane_scatter(q_all, q1_buf, 5)

    for step in (4, "4b"):
        ring[step].wait_send()
    for copy in across.values():
        copy.wait_send()
    p_plane.wait_send()
    g_line.wait_recv()
    gram[my_rows(core), :] = summed(g_src[core], g_buf, LINE)
    g_plane = plane_gather(gram, 4)
    s = dot_nt(r_cat[:n_rows, :], piv_cat[...])
    cross_own[...] = amp * matern(s + twice(r_norm[:n_rows, :]) + piv_norm_row)
    hi, lo = split(pv * -2.0)
    s = dot_nt(jnp.concatenate([hi, hi, lo], axis=1), piv_cat[...])
    full[...] = (noise * amp) * matern(s + twice(piv_norm) + piv_norm_row)

    g_line.wait_send()
    q1.wait_recv()
    q_src[...] = summed(q_all[:, here], q1_buf, PLANE)
    q_line = line_reduce(q_src, q_buf, 6)
    g_plane.wait_recv()
    r_copies = []
    for dx, dy in plane_offsets:
        k = dy * NX + dx
        source = part.at[pl.ds(k * n_rows, n_rows)]
        r_copies.append((source, prod_buf.at[k], plane(-dx, -dy)[0]))
    r_stage = stage(r_copies, 8, prod_buf.at[pl.ds(1, PLANE - 1)])
    full[...] = full[...] + gram[...]

    half = rank // 2
    tiles = half // 8
    work[...] = full[:half, :half].reshape(tiles, 8, half)
    invert(work)
    q_line.wait_recv()
    q_out[my_rows(core), :] = summed(q_src[core], q_buf, LINE)
    q_plane = plane_gather(q_out, 7)
    upper_inverse = work[...].reshape(half, half)
    lower = full[half:, :half]
    carried = dot_exact(upper_inverse, full[:half, half:])
    work[...] = (full[half:, half:] - dot_exact(lower, carried)).reshape(tiles, 8, half)
    invert(work)
    for later in (g_plane, q1, q_line, r_stage):
        later.wait_send()
    q_plane.wait_recv()
    lower_inverse = work[...].reshape(half, half)

    def solved(right_side):
        top = dot_exact(upper_inverse, right_side[:half])
        below = dot_exact(lower_inverse, right_side[half:] - dot_exact(lower, top))
        return jnp.concatenate([top - dot_exact(carried, below), below], axis=0)

    projected = q_out[...]
    coefficients = solved(projected)
    coefficients = coefficients + solved(projected - dot_exact(full[...], coefficients))
    r_stage.wait_recv()
    product_ref[...] = summed(prod_buf[1], prod_buf.at[pl.ds(1, PLANE - 1)], PLANE - 1)
    own_ref[...] = part[:n_rows, :]
    out_ref[...] = dot_exact(cross_own[...], coefficients)

    q_plane.wait_send()


def per_device(features, probes, outputscale, noise, pivots):
    n_rows, n_feat = features.shape
    n_probe = probes.shape[1]
    rank = pivots.shape[0]
    chunk = rank // NC // PLANE
    wide = PLANE * n_rows
    block = 4 * n_rows
    vmem = pltpu.VMEM
    dma = pltpu.SemaphoreType.DMA
    spread = jnp.broadcast_to(pivots[:, None], (rank, 128))
    others, own, removed = pl.pallas_call(
        exchange_kernel,
        out_shape=(jax.ShapeDtypeStruct((n_rows, n_probe), f32),) * 3,
        in_specs=[pl.BlockSpec(memory_space=vmem)] * 3
        + [pl.BlockSpec(memory_space=pltpu.SMEM)] * 2,
        out_specs=[pl.BlockSpec(memory_space=vmem)] * 3,
        scratch_shapes=[
            vmem((2, NY, NX, n_rows, n_feat // 2), f32),
            vmem((LINE, n_rows, n_feat + n_probe), f32),
            vmem((NC, PLANE, chunk, n_feat), f32),
            vmem((PLANE, NC, chunk, n_feat), f32),
            vmem((NC, chunk, n_feat), f32),
            vmem((LINE, chunk, n_feat), f32),
            vmem((rank, n_feat), f32),
            vmem((wide, 3 * n_feat), bf16),
            vmem((wide, 128), f32),
            vmem((1, wide), f32),
            vmem((block, 3 * n_feat), bf16),
            vmem((1, block), f32),
            vmem((block, 2 * n_probe), bf16),
            vmem((wide, n_probe), f32),
            vmem((rank, 3 * n_feat), bf16),
            vmem((rank, wide), f32),
            vmem((rank, wide), bf16),
            vmem((rank, wide), bf16),
            vmem((n_rows, rank), f32),
            vmem((NC, chunk, rank), f32),
            vmem((LINE, chunk, rank), f32),
            vmem((rank, rank), f32),
            vmem((NC, PLANE, chunk, n_probe), f32),
            vmem((PLANE, NC, chunk, n_probe), f32),
            vmem((NC, chunk, n_probe), f32),
            vmem((LINE, chunk, n_probe), f32),
            vmem((rank, n_probe), f32),
            vmem((PLANE, n_rows, n_probe), f32),
            vmem((rank // 16, 8, rank // 2), f32),
            vmem((rank, rank), f32),
            dma((2, 2 * PLANE)),
            dma((2, LINE + 1)),
            dma((2, 9)),
        ],
        compiler_params=pltpu.CompilerParams(
            collective_id=0, has_side_effects=True, vmem_limit_bytes=40 * 1024 * 1024
        ),
        name="exchange",
    )(features, probes, spread, outputscale, noise)
    product = own + others
    return product, (product - removed) / noise[0]


def solution(mesh):
    in_specs = (P(("blk", "row"), None), P(("blk", "row"), None), P(), P(), P())
    out_specs = (P(("blk", "row"), None), P(("blk", "row"), None))
    return jax.shard_map(
        per_device, mesh=mesh, in_specs=in_specs, out_specs=out_specs, check_vma=False
    )
```

```python
import jax
import jax.numpy as jnp
from jax import lax
from jax.experimental import pallas as pl
from jax.experimental.pallas import tpu as pltpu
from jax.sharding import PartitionSpec as P

MESH = pl.DeviceIdType.MESH
highest = lax.Precision.HIGHEST
root_five = 2.23606797749979
f32 = jnp.float32
bf16 = jnp.bfloat16

NX, NY, NZ, NC = 4, 4, 8, 2
ZLO = 4
PLANE = NX * NY
LINE = NZ * NC


def split(x):
    hi = x.astype(bf16)
    return hi, (x - hi.astype(f32)).astype(bf16)


def dot_nt(a, b):
    return lax.dot_general(a, b, (((1,), (1,)), ((), ())), preferred_element_type=f32)


def dot_nn(a, b):
    return jnp.dot(a, b, preferred_element_type=f32)


def matern(scaled_square):
    s = jnp.maximum(scaled_square, 1e-30)
    t = s * lax.rsqrt(s)
    return (1.0 + t + s * (1.0 / 3.0)) * jnp.exp(-t)


def column_norms(x):
    return jnp.broadcast_to(jnp.sum(x * x, axis=1, keepdims=True), (x.shape[0], 128))


def as_row(norms):
    return jnp.transpose(norms)[0:1]


def twice(x):
    return jnp.concatenate([x, x], axis=1)


def dot_exact(a, b):
    return jnp.dot(a, b, precision=highest, preferred_element_type=f32)


def invert(work):
    tiles, _, half = work.shape
    sub = lax.broadcasted_iota(jnp.int32, (8, half), 0)
    lane = lax.broadcasted_iota(jnp.int32, (8, half), 1)

    def spread_lane(v, c):
        return jnp.take_along_axis(v, jnp.full((8, half), c, jnp.int32), axis=1)

    def spread_row(v, r):
        return jnp.broadcast_to(v[r:r + 1, :], v.shape)

    def reciprocal(d):
        r = pl.reciprocal(d, approx=True)
        r = r * (2.0 - d * r)
        return r * (2.0 - d * r)

    def in_block(block):
        return (lane >= block * 8) & (lane < block * 8 + 8)

    def eliminated(top, block):
        d = [spread_lane(top, 8 * block + c) for c in range(8)]
        top = jnp.where(in_block(block), jnp.where(lane - block * 8 == sub, 1.0, 0.0), top)
        for s in range(0, 8, 2):
            a, b, c = spread_row(d[s], s), spread_row(d[s + 1], s), spread_row(d[s + 1], s + 1)
            inverse = reciprocal(a * c - b * b)
            first, second = d[s], d[s + 1]

            def swept(v):
                r0, r1 = spread_row(v, s), spread_row(v, s + 1)
                n0 = c * r0 - b * r1
                n1 = a * r1 - b * r0
                taken = jnp.where(sub == s, n0, jnp.where(sub == s + 1, n1, -(first * n0 + second * n1)))
                kept = jnp.where((sub == s) | (sub == s + 1), 0.0, v)
                return kept + taken * inverse

            for c2 in range(s + 2, 8):
                d[c2] = swept(d[c2])
            top = swept(top)
        return top

    def updated(v, block, rows):
        total = jnp.where(in_block(block), 0.0, v)
        for c in range(8):
            total = total - spread_lane(v, 8 * block + c) * rows[c]
        return total

    panel = tiles // 4
    for p in range(0, tiles, panel):
        block_rows = [work[p + i] for i in range(panel)]
        for i in range(panel):
            done = eliminated(block_rows[i], p + i)
            rows = [spread_row(done, c) for c in range(8)]
            for other in range(panel):
                if other != i:
                    block_rows[other] = updated(block_rows[other], p + i, rows)
            block_rows[i] = done
        reduced = jnp.concatenate(block_rows, axis=0)
        whole = work[...].reshape(half, half)
        first, last = 8 * p, 8 * (p + panel)
        column = lax.broadcasted_iota(jnp.int32, (half, half), 1)
        rest = jnp.where((column >= first) & (column < last), 0.0, whole)
        rest = rest - dot_exact(whole[:, first:last], reduced)
        work[...] = rest.reshape(tiles, 8, half)
        for i in range(panel):
            work[p + i] = block_rows[i]


def exchange_kernel(
    feats_ref, probes_ref, pivots_ref, amp_ref, noise_ref,
    product_ref, own_ref, out_ref,
    a_buf, b_buf, pick, p1_buf, p_src, p_buf, piv,
    r_cat, r_norm, r_norm_row, c_cat, c_norm_row, v_cat, part,
    piv_cat, ct, ct_hi, ct_lo, cross_own, g_src, g_buf, gram, q_all, q1_buf, q_src, q_buf, q_out, prod_buf, work, full,
    a_sem, b_sem, stage_sem,
):
    n_rows, n_feat = feats_ref.shape
    n_probe = probes_ref.shape[1]
    rank = pivots_ref.shape[0]
    half_rank = rank // NC
    chunk = half_rank // PLANE
    half_feat = n_feat // 2
    blk, row = lax.axis_index("blk"), lax.axis_index("row")
    core = lax.rem(blk, NC)
    y = lax.rem(lax.div(blk, NC), NY)
    x = lax.rem(row, NX)
    z = lax.div(row, NX) * ZLO + lax.div(blk, NC * NY)
    here = y * NX + x

    def plane(dx, dy):
        xx, yy = lax.rem(x + (dx + NX), NX), lax.rem(y + (dy + NY), NY)
        return ((lax.div(blk, NC * NY) * NY + yy) * NC + core, lax.div(row, NX) * NX + xx), yy * NX + xx

    def line(dz, dc):
        zz, cc = lax.rem(z + (dz + NZ), NZ), lax.rem(core + dc, NC)
        return ((lax.rem(zz, ZLO) * NY + y) * NC + cc, lax.div(zz, ZLO) * NX + x), cc

    plane_offsets = sorted(
        [(dx, dy) for dx in range(NX) for dy in range(NY) if dx or dy],
        key=lambda o: -(min(o[0], NX - o[0]) + min(o[1], NY - o[1])),
    )
    line_offsets = sorted(
        [(dz, dc) for dz in range(NZ) for dc in range(NC) if dz or dc],
        key=lambda o: -min(o[0], NZ - o[0]),
    )

    def send(src, dst, sem, k, device):
        copy = pltpu.make_async_remote_copy(
            src_ref=src, dst_ref=dst, send_sem=sem.at[0, k], recv_sem=sem.at[1, k],
            device_id=device, device_id_type=MESH,
        )
        copy.start()
        return copy

    barrier = pltpu.get_barrier_semaphore()
    for dx, dy in plane_offsets:
        pl.semaphore_signal(barrier, inc=1, device_id=plane(dx, dy)[0], device_id_type=MESH)
    for dz, dc in line_offsets:
        pl.semaphore_signal(barrier, inc=1, device_id=line(dz, dc)[0], device_id_type=MESH)

    amp, noise = amp_ref[0], noise_ref[0]
    own = feats_ref[...] * root_five
    a_buf[0, 0, 0] = own[:, :half_feat]
    a_buf[1, 0, 0] = own[:, half_feat:]
    b_buf[0, :, :n_feat] = own
    b_buf[0, :, n_feat:] = probes_ref[...]
    first = (blk * (NX * NZ // ZLO) + row) * n_rows
    point = lax.broadcasted_iota(jnp.int32, (rank, n_rows), 1) + first
    onehot = (point == pivots_ref[:, :n_rows]).astype(f32)
    pick[...] = dot_exact(onehot, own).reshape(NC, PLANE, chunk, n_feat)
    pl.semaphore_wait(barrier, PLANE + LINE - 2)

    upper_rows, lower_rows = pl.ds(0, n_rows // 2), pl.ds(n_rows // 2, n_rows // 2)

    moved = {}

    def a_slot(h, u, v):
        return a_buf.at[(h, v, u) if h == 0 else (h, u, v)]

    def a_send(h, u, v, du, dv):
        to = ((u + du) % 4, (v + dv) % 4)
        device = plane(du, dv)[0] if h == 0 else plane(dv, du)[0]
        moved[(h, *to)] = send(a_slot(h, u, v), a_slot(h, *to), a_sem, 16 * h + 4 * to[0] + to[1], device)

    def a_wait(*slots):
        for u, v in slots:
            for h in range(2):
                moved[(h, u, v)].wait_recv()

    def a_start():
        for d in (1, -1, 2):
            for h in range(2):
                a_send(h, 0, 0, d, 0)
                a_send(h, 0, 0, 0, d)

    def a_forward(*steps):
        for d in (1, -1, 2):
            for h in range(2):
                for u in steps:
                    a_send(h, u, 0, 0, d)

    right, left = line(1, 0)[0], line(-1, 0)[0]
    sibling = line(0, 1)[0]

    def b_slot(dz, dc):
        return b_buf.at[dz * NC + dc]

    def b_send(dz_from, dz_to, device):
        return send(b_slot(dz_from, 0), b_slot(dz_to, 0), b_sem, dz_to * NC, device)

    def b_sibling(dz):
        return send(b_slot(dz, 0), b_slot(dz, 1), b_sem, dz * NC + 1, sibling)

    def forward(step):
        ring[step].wait_recv()
        ring[8 - step].wait_recv()
        if step < 3:
            ring[step + 1] = b_send(step, step + 1, right)
            ring[7 - step] = b_send(8 - step, 7 - step, left)
        else:
            ring[4] = send(b_slot(3, 0).at[upper_rows], b_slot(4, 0).at[upper_rows], b_sem, 8, right)
            ring["4b"] = send(b_slot(5, 0).at[lower_rows], b_slot(4, 0).at[lower_rows], b_sem, LINE, left)
        across[step] = b_sibling(step)
        across[8 - step] = b_sibling(8 - step)

    def prepare(slots):
        for dx, dy in slots:
            k = dy * NX + dx
            rows = slice(k * n_rows, (k + 1) * n_rows)
            total = None
            for h in range(2):
                value = a_buf[h, dy, dx]
                hi, lo = split(value * -2.0)
                r_cat[rows, h * half_feat:(h + 1) * half_feat] = hi
                r_cat[rows, n_feat + h * half_feat:n_feat + (h + 1) * half_feat] = hi
                r_cat[rows, 2 * n_feat + h * half_feat:2 * n_feat + (h + 1) * half_feat] = lo
                square = value * value
                total = square if total is None else total + square
            r_norm[rows, :] = jnp.broadcast_to(jnp.sum(total, axis=1, keepdims=True), (n_rows, 128))

    def my_rows(c):
        return pl.ds(pl.multiple_of(c * half_rank + here * chunk, chunk), chunk)

    def stage(copies, number, whole):
        for src, dst, device in copies:
            pltpu.make_async_remote_copy(
                src_ref=src, dst_ref=dst, send_sem=stage_sem.at[0, number], recv_sem=stage_sem.at[1, number],
                device_id=device, device_id_type=MESH,
            ).start()
        return pltpu.make_async_remote_copy(
            src_ref=whole, dst_ref=whole, send_sem=stage_sem.at[0, number], recv_sem=stage_sem.at[1, number],
            device_id=sibling, device_id_type=MESH,
        )

    def line_reduce(src, dst, number):
        copies = []
        for dz, dc in line_offsets:
            device, cc = line(dz, dc)
            copies.append((src.at[cc], dst.at[dz * NC + dc], device))
        return stage(copies, number, dst.at[pl.ds(1, LINE - 1)])

    def plane_gather(ref, number):
        copies = []
        mine = ref.at[my_rows(core)]
        for dx, dy in plane_offsets:
            (other_blk, other_row), _ = plane(dx, dy)
            copies.append((mine, mine, (other_blk, other_row)))
            copies.append((mine, mine, (other_blk + 1 - 2 * core, other_row)))
        copies.append((mine, mine, sibling))
        return stage(copies, number, ref.at[pl.ds(0, len(copies) * chunk)])

    def plane_scatter(src, dst, number):
        copies = []
        for dx, dy in plane_offsets:
            device, there = plane(dx, dy)
            copies.append((src.at[:, there], dst.at[dy * NX + dx], device))
        return stage(copies, number, dst.at[pl.ds(1, PLANE - 1)])

    def summed(total, buf, count):
        for k in range(1, count):
            total = total + buf[k]
        return total

    p_scatter = plane_scatter(pick, p1_buf, 0)
    ring = {1: b_send(0, 1, right), 7: b_send(0, 7, left)}
    across = {0: b_sibling(0)}
    a_start()
    prepare([(0, 0)])
    a_wait((1, 0), (3, 0))
    a_forward(1, 3)
    forward(1)
    p_scatter.wait_recv()
    p_src[...] = summed(pick[:, here], p1_buf, PLANE)
    p_line = line_reduce(p_src, p_buf, 1)
    a_wait((2, 0))
    a_forward(2)
    a_wait((0, 1), (0, 3), (0, 2))
    prepare([(1, 0), (3, 0), (2, 0), (0, 1), (0, 3), (0, 2)])
    forward(2)
    p_line.wait_recv()
    piv[my_rows(core), :] = summed(p_src[core], p_buf, LINE)
    p_plane = plane_gather(piv, 2)
    a_wait((1, 1), (1, 3), (3, 1), (3, 3), (1, 2), (3, 2), (2, 1), (2, 3), (2, 2))
    prepare([(1, 1), (1, 3), (3, 1), (3, 3), (2, 1), (2, 3), (1, 2), (3, 2), (2, 2)])
    forward(3)

    for k in range(0, r_norm.shape[0], 128):
        r_norm_row[:, k:k + 128] = as_row(r_norm[k:k + 128, :])
    part[...] = jnp.zeros_like(part)
    tile = 256

    def columns(slots):
        for i, (dz, dc) in enumerate(slots):
            rows = slice(i * n_rows, (i + 1) * n_rows)
            value = b_buf[dz * NC + dc, :, :n_feat]
            hi, lo = split(value)
            c_cat[rows, :n_feat] = hi
            c_cat[rows, n_feat:2 * n_feat] = lo
            c_cat[rows, 2 * n_feat:] = hi
            hi, lo = split(b_buf[dz * NC + dc, :, n_feat:])
            v_cat[rows, :n_probe] = hi
            v_cat[rows, n_probe:] = lo
        for i in range(0, len(slots), 2):
            pair = [column_norms(b_buf[dz * NC + dc, :, :n_feat]) for dz, dc in slots[i:i + 2]]
            c_norm_row[:, i * n_rows:(i + 2) * n_rows] = as_row(jnp.concatenate(pair, axis=0))

        def body(i, carry):
            rows = pl.ds(pl.multiple_of(i * tile, tile), tile)
            s = dot_nt(r_cat[rows, :], c_cat[...])
            k = matern(s + twice(r_norm[rows, :]) + c_norm_row[...])
            hi, lo = split(k)
            both = dot_nn(hi, v_cat[...])
            last = dot_nn(lo, v_cat[:, :n_probe])
            part[rows, :] = part[rows, :] + (both[:, :n_probe] + both[:, n_probe:] + last)
            return carry

        lax.fori_loop(0, part.shape[0] // tile, body, 0, unroll=4)

    across[0].wait_recv()
    across[1].wait_recv()
    columns([(0, 0), (0, 1), (1, 0), (1, 1)])

    across[2].wait_recv()
    across[7].wait_recv()
    columns([(7, 0), (7, 1), (2, 0), (2, 1)])
    for c in list(moved.values()) + [ring[k] for k in (1, 2, 3, 5, 6, 7)]:
        c.wait_send()
    p_scatter.wait_send()
    p_line.wait_send()
    p_plane.wait_recv()
    pv = piv[...]
    hi, lo = split(pv)
    piv_cat[:, :n_feat] = hi
    piv_cat[:, n_feat:2 * n_feat] = lo
    piv_cat[:, 2 * n_feat:] = hi
    piv_norm = column_norms(pv)
    piv_norm_row = jnp.concatenate([as_row(piv_norm[k:k + 128]) for k in range(0, rank, 128)], axis=1)
    for i in range(r_cat.shape[0] // tile):
        rows = slice(i * tile, (i + 1) * tile)
        s = dot_nt(piv_cat[...], r_cat[rows, :])
        value = amp * matern(s + twice(piv_norm) + r_norm_row[:, rows])
        ct[:, rows] = value
        hi, lo = split(value)
        ct_hi[:, rows] = hi
        ct_lo[:, rows] = lo
    hi, lo = split(jnp.concatenate([ct[my_rows(c), :] for c in range(NC)], axis=0))
    both = dot_nt(jnp.concatenate([hi, lo], axis=0), ct_hi[...])
    g = both[:NC * chunk] + both[NC * chunk:] + dot_nt(hi, ct_lo[...])
    g_src[...] = g.reshape(NC, chunk, rank)
    g_line = line_reduce(g_src, g_buf, 3)

    ring[4].wait_recv()
    ring["4b"].wait_recv()
    across[4] = b_sibling(4)
    across[6].wait_recv()
    across[3].wait_recv()
    columns([(6, 0), (6, 1), (3, 0), (3, 1)])
    across[5].wait_recv()
    across[4].wait_recv()
    columns([(5, 0), (5, 1), (4, 0), (4, 1)])

    part[...] = part[...] * amp
    part[:n_rows, :] = part[:n_rows, :] + noise * probes_ref[...]
    hi, lo = split(part[...])
    both = dot_nn(ct_hi[...], jnp.concatenate([hi, lo], axis=1))
    q = both[:, :n_probe] + both[:, n_probe:] + dot_nn(ct_lo[...], hi)
    q_all[...] = q.reshape(NC, PLANE, chunk, n_probe)
    q1 = plane_scatter(q_all, q1_buf, 5)

    for step in (4, "4b"):
        ring[step].wait_send()
    for copy in across.values():
        copy.wait_send()
    p_plane.wait_send()
    g_line.wait_recv()
    gram[my_rows(core), :] = summed(g_src[core], g_buf, LINE)
    g_plane = plane_gather(gram, 4)
    s = dot_nt(r_cat[:n_rows, :], piv_cat[...])
    cross_own[...] = amp * matern(s + twice(r_norm[:n_rows, :]) + piv_norm_row)
    hi, lo = split(pv * -2.0)
    s = dot_nt(jnp.concatenate([hi, hi, lo], axis=1), piv_cat[...])
    full[...] = (noise * amp) * matern(s + twice(piv_norm) + piv_norm_row)

    g_line.wait_send()
    q1.wait_recv()
    q_src[...] = summed(q_all[:, here], q1_buf, PLANE)
    q_line = line_reduce(q_src, q_buf, 6)
    g_plane.wait_recv()
    r_copies = []
    for dx, dy in plane_offsets:
        k = dy * NX + dx
        source = part.at[pl.ds(k * n_rows, n_rows)]
        r_copies.append((source, prod_buf.at[k], plane(-dx, -dy)[0]))
    r_stage = stage(r_copies, 8, prod_buf.at[pl.ds(1, PLANE - 1)])
    full[...] = full[...] + gram[...]

    half = rank // 2
    tiles = half // 8
    work[...] = full[:half, :half].reshape(tiles, 8, half)
    invert(work)
    q_line.wait_recv()
    q_out[my_rows(core), :] = summed(q_src[core], q_buf, LINE)
    q_plane = plane_gather(q_out, 7)
    upper_inverse = work[...].reshape(half, half)
    lower = full[half:, :half]
    carried = dot_exact(upper_inverse, full[:half, half:])
    work[...] = (full[half:, half:] - dot_exact(lower, carried)).reshape(tiles, 8, half)
    invert(work)
    for later in (g_plane, q1, q_line, r_stage):
        later.wait_send()
    q_plane.wait_recv()
    lower_inverse = work[...].reshape(half, half)

    def solved(right_side):
        top = dot_exact(upper_inverse, right_side[:half])
        below = dot_exact(lower_inverse, right_side[half:] - dot_exact(lower, top))
        return jnp.concatenate([top - dot_exact(carried, below), below], axis=0)

    projected = q_out[...]
    coefficients = solved(projected)
    coefficients = coefficients + solved(projected - dot_exact(full[...], coefficients))
    r_stage.wait_recv()
    product_ref[...] = summed(prod_buf[1], prod_buf.at[pl.ds(1, PLANE - 1)], PLANE - 1)
    own_ref[...] = part[:n_rows, :]
    out_ref[...] = dot_exact(cross_own[...], coefficients)

    q_plane.wait_send()


def per_device(features, probes, outputscale, noise, pivots):
    n_rows, n_feat = features.shape
    n_probe = probes.shape[1]
    rank = pivots.shape[0]
    chunk = rank // NC // PLANE
    wide = PLANE * n_rows
    block = 4 * n_rows
    vmem = pltpu.VMEM
    dma = pltpu.SemaphoreType.DMA
    spread = jnp.broadcast_to(pivots[:, None], (rank, 128))
    others, own, removed = pl.pallas_call(
        exchange_kernel,
        out_shape=(jax.ShapeDtypeStruct((n_rows, n_probe), f32),) * 3,
        in_specs=[pl.BlockSpec(memory_space=vmem)] * 3
        + [pl.BlockSpec(memory_space=pltpu.SMEM)] * 2,
        out_specs=[pl.BlockSpec(memory_space=vmem)] * 3,
        scratch_shapes=[
            vmem((2, NY, NX, n_rows, n_feat // 2), f32),
            vmem((LINE, n_rows, n_feat + n_probe), f32),
            vmem((NC, PLANE, chunk, n_feat), f32),
            vmem((PLANE, NC, chunk, n_feat), f32),
            vmem((NC, chunk, n_feat), f32),
            vmem((LINE, chunk, n_feat), f32),
            vmem((rank, n_feat), f32),
            vmem((wide, 3 * n_feat), bf16),
            vmem((wide, 128), f32),
            vmem((1, wide), f32),
            vmem((block, 3 * n_feat), bf16),
            vmem((1, block), f32),
            vmem((block, 2 * n_probe), bf16),
            vmem((wide, n_probe), f32),
            vmem((rank, 3 * n_feat), bf16),
            vmem((rank, wide), f32),
            vmem((rank, wide), bf16),
            vmem((rank, wide), bf16),
            vmem((n_rows, rank), f32),
            vmem((NC, chunk, rank), f32),
            vmem((LINE, chunk, rank), f32),
            vmem((rank, rank), f32),
            vmem((NC, PLANE, chunk, n_probe), f32),
            vmem((PLANE, NC, chunk, n_probe), f32),
            vmem((NC, chunk, n_probe), f32),
            vmem((LINE, chunk, n_probe), f32),
            vmem((rank, n_probe), f32),
            vmem((PLANE, n_rows, n_probe), f32),
            vmem((rank // 16, 8, rank // 2), f32),
            vmem((rank, rank), f32),
            dma((2, 2 * PLANE)),
            dma((2, LINE + 1)),
            dma((2, 9)),
        ],
        compiler_params=pltpu.CompilerParams(
            collective_id=0, has_side_effects=True, vmem_limit_bytes=40 * 1024 * 1024
        ),
        name="exchange",
    )(features, probes, spread, outputscale, noise)
    product = own + others
    return product, (product - removed) / noise[0]


def solution(mesh):
    in_specs = (P(("blk", "row"), None), P(("blk", "row"), None), P(), P(), P())
    out_specs = (P(("blk", "row"), None), P(("blk", "row"), None))
    return jax.shard_map(
        per_device, mesh=mesh, in_specs=in_specs, out_specs=out_specs, check_vma=False
    )
```
